32 devices in a mesh: rec: 4 (over z), ani: 4 (over x, core), chain: 2 (over y).
Axes of the slice: x: 2, y: 2, z: 4, core: 2. Of those that a mesh axis runs over, the one named last changes fastest.
Arguments:
- genotypes: bfloat16 [131072, 4096], P('ani', 'rec'), may hold values from -0.09375 to 0.09375
- effects: float32 [8192], P(('chain', 'rec')), parts along dimension 0, may hold values from -6 to 6
- gaussian_draw: float32 [8192], P(('chain', 'rec')), parts along dimension 0, may hold values from -6 to 6
- prior_prec: float32 [4096], P('rec'), may hold values from 2 to 40
- accept: int32 [64], P(('chain', 'rec')), parts along dimension 0, may hold values 0 or 1
- herd_effect: float32 [16384], P(('chain', 'rec')), parts along dimension 0, may hold values from -6 to 6
- phenotype: float32 [131072], P(('rec', 'ani')), may hold values from -12 to 12
- record_animal: int32 [131072], P(('rec', 'ani')), may hold values from 0 to 131071
- record_bin: int32 [131072], P(('rec', 'ani')), may hold values from 0 to 8191, as said below
- live_records: int32 [16], P(('rec', 'ani')), may hold values from 1 to 8192, 81920 in all
Outputs:
- next_effects: float32 [8192], P(('chain', 'rec')), parts along dimension 0
- resid_sum: float32 [262144], P(('chain', 'ani')), parts along dimension 0
The draws below stay inside these ranges and needn't reach their ends.
There are 2 independent parts, one for each index of `chain`. The reference program is written for one: setup_inputs(seed, part) draws one part's arguments, and reference() takes and returns one part's arrays. A program takes and returns all parts, laid end to end along the dimension named above; an argument that names none is the same for every part. Nothing has to cross between parts.
Inputs may be any that keep to these rules, and one draw needn't show every extreme that they name: `record_bin`: a record held by rec index k names a group of k * 2048 to (k + 1) * 2048 - 1.
All inputs are finite; a program needn't handle non-finite values. No bound on the sum of `accept` or of `live_records` on one device may be relied on, other than what follows from the above.
Results may differ from the reference program's by a relative error of at most 0.0033.
Values sent between devices are 32-bit elements; how exact they have to be, the bound alone decides.
No kernel may reach another device: no remote copies, remote signals or barrier semaphores. Data moves between devices by JAX's collectives and lax.ppermute only.
A program may use at most 128 MiB of HBM per device.

```python
import math
import jax
import jax.numpy as jnp
import numpy as np

M = 4096
BLOCK = 128
RD = 8192
HB = 2048
ANIMALS = 131072
SHARD_RECS = 32768
RECORDS = 131072
BINS = 8192
N_REC = 4
N_ANI = 4


def draw_record_bin(key, part):
    position = jnp.arange(RECORDS, dtype=jnp.int32)
    shard = position // SHARD_RECS
    offset = jax.random.randint(key, (RECORDS,), 0, HB, dtype=jnp.int32)
    return shard * HB + offset


def touch_ends(array, stream_key, smallest, high):
    longest = array.shape.index(max(array.shape))
    spots = []
    for shift in (0, 1):
        where = [jax.random.randint(jax.random.fold_in(stream_key, axis), (), 0, length) for axis, length in enumerate(array.shape)]
        where[longest] = (where[longest] + shift) % array.shape[longest]
        spots.append(tuple(where))
    return array.at[spots[0]].set(smallest).at[spots[1]].set(high)


def levels(rng, extent, cuts, least, largest):
    loudness = 1.0
    for dim, blocks in cuts:
        heights = jax.random.uniform(jax.random.fold_in(jax.random.fold_in(rng, 6), dim), (blocks,), jnp.float32, least / len(cuts), largest / len(cuts))
        loudness = loudness * jnp.repeat(jnp.exp(heights), extent[dim] // blocks).reshape((-1,) + (1,) * (len(extent) - 1 - dim))
    return loudness


def length_profile(number_of, total, bound, slope):
    portions = [(1 << 20) // math.isqrt(standing ** slope) + 1 for standing in range(2, number_of + 1)]
    spare, given = total - bound - (number_of - 1), [1] * (number_of - 1)
    while spare > 0:
        free = [i for i in range(number_of - 1) if given[i] < bound]
        whole, left = sum([portions[i] for i in free]), spare
        for i in free:
            more = min(bound - given[i], max(1, left * portions[i] // whole), spare)
            given[i] = given[i] + more
            spare = spare - more
    return np.array([bound] + given)


def ragged(stream_key, amount, total, reach, skew):
    if amount == 2:
        one = jax.random.randint(stream_key, (), max(1, total - reach), min(reach, total - 1) + 1)
        return jnp.stack([one, total - one])
    tallies = jnp.asarray(length_profile(amount, total, reach, skew), jnp.int32)
    pairs = (amount - 1) // 2
    source_of, sink = tallies[1:1 + 2 * pairs:2], tallies[2:2 + 2 * pairs:2]
    margin = jnp.minimum(source_of - 1, reach - sink)
    passed = jax.random.randint(jax.random.fold_in(stream_key, 1), (pairs,), 0, 1 << 20) % (margin + 1)
    tallies = tallies.at[1:1 + 2 * pairs:2].set(source_of - passed).at[2:2 + 2 * pairs:2].set(sink + passed)
    return tallies[jax.random.permutation(jax.random.fold_in(stream_key, 2), amount)]


def noise(key, dims, spread, limit, cuts=(), kind=jnp.bfloat16):
    result = jax.random.normal(key, dims, jnp.float32) * spread
    if len(cuts) > 0:
        result = levels(key, dims, cuts, -0.22, 0.18) * result
    return jnp.clip(result, min=-limit, max=limit).astype(kind)


def setup_inputs(seed: int = 0, part: int = 0) -> dict:
    key_list = jax.random.split(jax.random.key(seed), 11)
    part_keys = jax.random.split(jax.random.fold_in(key_list[10], part), 11)
    return {
        "genotypes": noise(key_list[0], (ANIMALS, M), M ** -0.5, 0.09375, ((0, 4), (1, 4))),
        "effects": noise(part_keys[1], (M,), 1.0, 6.0, ((0, 4),), jnp.float32),
        "gaussian_draw": noise(part_keys[2], (M,), 1.0, 6.0, ((0, 4),), jnp.float32),
        "prior_prec": jnp.clip(jnp.exp(math.log(40.0) - 2.9957323 * jax.random.uniform(key_list[3], (M,), jnp.float32) ** levels(key_list[3], (M,), ((0, 4),), -0.2, 0.2)), 2.0, 40.0),
        "accept": touch_ends((jax.random.randint(part_keys[4], (M // BLOCK,), 0, 4) < 3).astype(jnp.int32), jax.random.fold_in(part_keys[4], 1), 0, 1),
        "herd_effect": noise(part_keys[5], (BINS,), 1.0, 6.0, ((0, 4),), jnp.float32),
        "phenotype": noise(key_list[6], (RECORDS,), 2.0, 12.0, ((0, 16),), jnp.float32),
        "record_animal": touch_ends(jax.random.randint(key_list[7], (RECORDS,), 0, ANIMALS), jax.random.fold_in(key_list[7], 1), 0, ANIMALS - 1).astype(jnp.int32),
        "record_bin": draw_record_bin(jax.random.fold_in(key_list[10], 71), part),
        "live_records": ragged(key_list[9], N_REC * N_ANI, RD * N_REC * N_ANI * 5 // 8, RD, 2).astype(jnp.int32),
    }


def reference(genotypes, effects, gaussian_draw, prior_prec, accept, herd_effect, phenotype, record_animal, record_bin, live_records):
    step_size = 0.005
    effects_half = effects.astype(jnp.bfloat16)
    breeding = jnp.dot(genotypes, effects_half, preferred_element_type=jnp.float32)
    position = jnp.arange(RECORDS, dtype=jnp.int32)
    live = position % RD < jnp.take(live_records, position // RD)
    residual = jnp.where(live, phenotype - jnp.take(herd_effect, record_bin) - jnp.take(breeding, record_animal), jnp.zeros_like(phenotype))
    resid_sum = jax.ops.segment_sum(residual, record_animal, num_segments=ANIMALS)
    resid_half = resid_sum.astype(jnp.bfloat16)
    gradient = jnp.dot(resid_half, genotypes, preferred_element_type=jnp.float32) - prior_prec * effects
    proposal = effects + step_size * gradient + math.sqrt(2.0 * step_size) * gaussian_draw
    accepted = jnp.repeat(accept, BLOCK) == 1
    return (jnp.where(accepted, proposal, effects), resid_sum)
```

```python
import functools
import math

import jax
import jax.numpy as jnp
from jax import lax
from jax.experimental import pallas as pl
from jax.experimental.pallas import tpu as pltpu
from jax.sharding import PartitionSpec as P

BLOCK = 128
LANES = 128
SUBS = 64
CHUNK_ROWS = 16
F32 = jnp.float32
BF16 = jnp.bfloat16
NT = (((1,), (1,)), ((), ()))


def permute(x, axis, size, shift):
    return lax.ppermute(x, axis, [(i, (i + shift) % size) for i in range(size)])


def product1_kernel(n, per, tile, where_ref, e_ref, g_ref, out_ref):
    step = pl.program_id(0)
    piece, part = step // per, step % per
    rows = out_ref.shape[1] // 2
    res = lax.dot_general(e_ref[...], g_ref[...], NT, preferred_element_type=F32)
    for i in range(tile // LANES):
        at = part * (tile // LANES) + i
        out_ref[piece, pl.ds(at, 1), :] = res[0:1, i * LANES : (i + 1) * LANES]
        out_ref[piece, pl.ds(rows + at, 1), :] = res[1:2, i * LANES : (i + 1) * LANES]


def product1(genotypes, e2, where, n, half):
    markers = genotypes.shape[1]
    quarter = half // n
    tile = min(quarter, 2048)
    per = quarter // tile
    rows = quarter // LANES

    def g_map(step, where_ref):
        chain, rec = where_ref[0], where_ref[1]
        piece, part = step // per, step % per
        return (chain * (half // tile) + lax.rem(rec + piece, n) * per + part, 0)

    return pl.pallas_call(
        functools.partial(product1_kernel, n, per, tile),
        grid_spec=pltpu.PrefetchScalarGridSpec(
            num_scalar_prefetch=1,
            grid=(n * per,),
            in_specs=[
                pl.BlockSpec((8, markers), lambda s, w: (0, 0)),
                pl.BlockSpec((tile, markers), g_map),
            ],
            out_specs=pl.BlockSpec((n, 2 * rows, LANES), lambda s, w: (0, 0, 0)),
        ),
        out_shape=jax.ShapeDtypeStruct((n, 2 * rows, LANES), F32),
        compiler_params=pltpu.CompilerParams(
            dimension_semantics=("arbitrary",), vmem_limit_bytes=32 << 20
        ),
        cost_estimate=pl.CostEstimate(
            flops=4 * half * markers, bytes_accessed=2 * half * markers, transcendentals=0
        ),
        name="product1",
    )(where, e2, genotypes)


def records_kernel(n, n_src, where_ref, herd_ref, b_ref, *refs):
    srcs, out_ref = refs[:n_src], refs[n_src]
    lane_s, sub_s, v_s, acc, tab = refs[n_src + 1 :]
    src_rows = srcs[0].shape[0] // 3
    bins = herd_ref.shape[1]
    base = where_ref[2]
    span = 2 * SUBS * LANES
    for k, src in enumerate(srcs):
        for g in range(src_rows // 8):
            at = pl.ds(k * src_rows + g * 8, 8)
            local = src[g * 8 : g * 8 + 8, :].astype(jnp.int32) - base
            y = src[src_rows + g * 8 : src_rows + g * 8 + 8, :]
            which = src[2 * src_rows + g * 8 : 2 * src_rows + g * 8 + 8, :].astype(jnp.int32)
            known = (local >= 0) & (local < span)
            lane = (local & (LANES - 1)) | ((local >> 13) << 7)
            lane_s[at, :] = jnp.where(known, lane, -1).astype(F32)
            sub_s[at, :] = ((local >> 7) & (SUBS - 1)).astype(F32)
            low, high = which & (LANES - 1), which >> 7
            for ch in range(2):
                found = jnp.zeros((8, LANES), F32)
                for t in range(bins):
                    row = jnp.broadcast_to(herd_ref[ch, t : t + 1, :], (8, LANES))
                    got = jnp.take_along_axis(row, low, axis=1, mode="promise_in_bounds")
                    found = jnp.where(high == t, got, found)
                value = y - found
                upper = value.astype(BF16).astype(F32)
                v_s[2 * ch, at, :] = upper
                v_s[2 * ch + 1, at, :] = value - upper
    acc[...] = jnp.zeros_like(acc)
    lanes_iota = lax.broadcasted_iota(jnp.int32, (2 * LANES, LANES), 0).astype(F32).astype(BF16)
    subs_iota = lax.broadcasted_iota(jnp.int32, (SUBS, LANES), 0).astype(F32).astype(BF16)

    def spread(ref_row, count):
        return jnp.broadcast_to(
            jnp.broadcast_to(ref_row, (16, LANES)).astype(BF16)[None], (count // 16, 16, LANES)
        ).reshape(count, LANES)

    def chunk(t, carry):
        a_cols, b_cols = [], []
        for i in range(CHUNK_ROWS):
            at = pl.ds(t * CHUNK_ROWS + i, 1)
            lane = spread(lane_s[at, :], 2 * LANES)
            a_cols.append(jnp.where(lanes_iota == lane, jnp.ones((), BF16), jnp.zeros((), BF16)))
            mask = subs_iota == spread(sub_s[at, :], SUBS)
            pieces = [
                jnp.where(mask, spread(v_s[p, at, :], SUBS), jnp.zeros((), BF16)) for p in range(4)
            ]
            pieces.append(jnp.where(mask, jnp.ones((), BF16), jnp.zeros((), BF16)))
            b_cols.append(jnp.concatenate(pieces, axis=0))
        acc[...] += lax.dot_general(
            jnp.concatenate(b_cols, axis=1),
            jnp.concatenate(a_cols, axis=1),
            NT,
            preferred_element_type=F32,
        )
        return carry

    lax.fori_loop(0, n_src * src_rows // CHUNK_ROWS, chunk, 0)
    rows = 2 * SUBS // n
    for q in range(n):
        wide, first = divmod(q * rows, SUBS)
        cols = slice(wide * LANES, (wide + 1) * LANES)
        window = lambda p: acc[p * SUBS + first : p * SUBS + first + rows, cols]
        tab[0, q] = window(0) + window(1)
        tab[1, q] = window(2) + window(3)
        tab[2, q] = window(4)
    for j in range(n):
        owner = lax.rem(where_ref[1] + j, n)
        out_ref[j, 0 : 2 * rows, :] = b_ref[j]
        for p in range(3):
            out_ref[j, (2 + p) * rows : (3 + p) * rows, :] = tab[p, owner]


def records(where, herd2, b, srcs, n):
    n_src = len(srcs)
    src_rows = srcs[0].shape[0] // 3
    total = n_src * src_rows
    rows = 2 * SUBS // n
    full = lambda x: pl.BlockSpec(x.shape, lambda: (0,) * x.ndim)
    return pl.pallas_call(
        functools.partial(records_kernel, n, n_src),
        in_specs=[pl.BlockSpec(memory_space=pltpu.SMEM), full(herd2), full(b)]
        + [full(s) for s in srcs],
        out_specs=pl.BlockSpec((n, 5 * rows, LANES), lambda: (0, 0, 0)),
        out_shape=jax.ShapeDtypeStruct((n, 5 * rows, LANES), F32),
        scratch_shapes=[
            pltpu.VMEM((total, LANES), F32),
            pltpu.VMEM((total, LANES), F32),
            pltpu.VMEM((4, total, LANES), F32),
            pltpu.VMEM((5 * SUBS, 2 * LANES), F32),
            pltpu.VMEM((3, n, rows, LANES), F32),
        ],
        compiler_params=pltpu.CompilerParams(vmem_limit_bytes=24 << 20),
        cost_estimate=pl.CostEstimate(
            flops=2 * total * LANES * 5 * SUBS * 2 * LANES,
            bytes_accessed=16 * total * LANES,
            transcendentals=0,
        ),
        name="records",
    )(where, herd2, b, *srcs)


def assemble_kernel(n, where_ref, *refs):
    parts, (own_ref, other_ref) = refs[:n], refs[n:]
    rows = parts[0].shape[0] // 2
    for j in range(n):
        owner = lax.rem(where_ref[1] + j, n)
        own_ref[owner] = parts[j][0:rows, :]
        other_ref[owner] = parts[j][rows : 2 * rows, :]


def assemble(where, parts, n):
    rows = parts[0].shape[0] // 2
    full = pl.BlockSpec(parts[0].shape, lambda: (0, 0))
    out = pl.BlockSpec((n, rows, LANES), lambda: (0, 0, 0))
    own, other = pl.pallas_call(
        functools.partial(assemble_kernel, n),
        in_specs=[pl.BlockSpec(memory_space=pltpu.SMEM)] + [full] * n,
        out_specs=[out, out],
        out_shape=[jax.ShapeDtypeStruct((n, rows, LANES), F32)] * 2,
        name="assemble",
    )(where, *parts)
    return own.reshape(n * rows, LANES), other.reshape(n * rows, LANES)


def product2_kernel(where_ref, own_ref, other_ref, g_ref, out_ref):
    step = pl.program_id(0)

    @pl.when(step == 0)
    def _():
        out_ref[...] = jnp.zeros_like(out_ref)

    rows = own_ref.shape[0]
    cols = []
    for i in range(rows):
        pair = jnp.concatenate([own_ref[i : i + 1, :], other_ref[i : i + 1, :]], axis=0)
        cols.append(jnp.concatenate([pair, jnp.zeros((6, LANES), F32)], axis=0))
    lhs = jnp.concatenate(cols, axis=1).astype(BF16)
    out_ref[...] += jnp.dot(lhs, g_ref[...], preferred_element_type=F32)


def product2(genotypes, own, other, where, half):
    markers = genotypes.shape[1]
    tile = min(half, 2048)
    spec = pl.BlockSpec((tile // LANES, LANES), lambda s, w: (s, 0))
    return pl.pallas_call(
        product2_kernel,
        grid_spec=pltpu.PrefetchScalarGridSpec(
            num_scalar_prefetch=1,
            grid=(half // tile,),
            in_specs=[
                spec,
                spec,
                pl.BlockSpec((tile, markers), lambda s, w: (w[0] * (half // tile) + s, 0)),
            ],
            out_specs=pl.BlockSpec((8, markers), lambda s, w: (0, 0)),
        ),
        out_shape=jax.ShapeDtypeStruct((8, markers), F32),
        compiler_params=pltpu.CompilerParams(
            dimension_semantics=("arbitrary",), vmem_limit_bytes=32 << 20
        ),
        cost_estimate=pl.CostEstimate(
            flops=4 * half * markers, bytes_accessed=2 * half * markers, transcendentals=0
        ),
        name="product2",
    )(where, own, other, genotypes)


def on_device(
    n_rec,
    n_ani,
    genotypes,
    effects,
    gaussian_draw,
    prior_prec,
    accept,
    herd_effect,
    phenotype,
    record_animal,
    record_bin,
    live_records,
):
    step_size = 0.005
    block, markers = genotypes.shape
    half = block // 2
    slots = phenotype.shape[0]
    bins = herd_effect.shape[0]
    chain, rec, ani = lax.axis_index("chain"), lax.axis_index("rec"), lax.axis_index("ani")
    where = jnp.stack([chain, rec, ani * block + chain * half]).astype(jnp.int32)

    mine = jnp.concatenate([effects, herd_effect])
    theirs = permute(mine, "chain", 2, 1)
    live = jnp.arange(slots, dtype=jnp.int32) < live_records[0]
    raw = jnp.concatenate(
        [
            jnp.where(live, record_animal, -1).astype(F32),
            phenotype,
            (record_bin - rec * bins).astype(F32),
        ]
    ).reshape(3 * slots // LANES, LANES)
    srcs = [raw] + [permute(raw, "ani", n_ani, k) for k in range(1, n_ani)]

    e2 = jnp.concatenate(
        [effects[None], theirs[None, :markers], jnp.zeros((6, markers), F32)]
    ).astype(BF16)
    herd2 = jnp.stack([herd_effect, theirs[markers:]]).reshape(2, bins // LANES, LANES)

    b = product1(genotypes, e2, where, n_rec, half)
    sums = records(where, herd2, b, srcs, n_rec)
    total = sums[0]
    for k in range(1, n_rec):
        total = total + permute(sums[k], "rec", n_rec, k)
    rows = half // n_rec // LANES
    count = total[4 * rows :]
    resid = total[2 * rows : 4 * rows] - jnp.concatenate([count, count]) * total[: 2 * rows]

    parts = [resid] + [permute(resid, "rec", n_rec, n_rec - k) for k in range(1, n_rec)]
    own, other = assemble(where, parts, n_rec)
    back = permute(other, "chain", 2, 1)
    grads = product2(genotypes, own, other, where, half)
    grad_part = grads[0] + permute(grads[1], "chain", 2, 1)
    resid_sum = jnp.where(
        chain == 0, jnp.concatenate([own, back]), jnp.concatenate([back, own])
    ).reshape(block)

    likelihood_grad = lax.psum(grad_part, "ani")
    gradient = likelihood_grad - prior_prec * effects
    proposal = effects + step_size * gradient + math.sqrt(2.0 * step_size) * gaussian_draw
    accepted = jnp.repeat(accept, BLOCK) == 1
    return (jnp.where(accepted, proposal, effects), resid_sum)


def solution(mesh):
    return jax.shard_map(
        functools.partial(on_device, mesh.shape["rec"], mesh.shape["ani"]),
        mesh=mesh,
        in_specs=(
            P("ani", "rec"),
            P(("chain", "rec")),
            P(("chain", "rec")),
            P("rec"),
            P(("chain", "rec")),
            P(("chain", "rec")),
            P(("rec", "ani")),
            P(("rec", "ani")),
            P(("rec", "ani")),
            P(("rec", "ani")),
        ),
        out_specs=(P(("chain", "rec")), P(("chain", "ani"))),
        check_vma=False,
    )
```

```python
import functools
import math

import jax
import jax.numpy as jnp
from jax import lax
from jax.experimental import pallas as pl
from jax.experimental.pallas import tpu as pltpu
from jax.sharding import PartitionSpec as P

BLOCK = 128
LANES = 128
SUBS = 64
SPAN_BITS = 14
CHUNK_ROWS = 16
TILE = 2048
F32 = jnp.float32
BF16 = jnp.bfloat16
NT = (((1,), (1,)), ((), ()))
VMEM = pl.BlockSpec(memory_space=pltpu.VMEM)
SMEM = pl.BlockSpec(memory_space=pltpu.SMEM)
ANY = pl.BlockSpec(memory_space=pl.ANY)


def permute(x, axis, size, shift):
    return lax.ppermute(x, axis, [(i, (i + shift) % size) for i in range(size)])


def tiled(x):
    return x.reshape(-1, LANES)


def prepare_kernel(live_ref, animal_ref, y_ref, bin_ref, e_ref, h_ref, raw_ref, mine_ref):
    rows = animal_ref.shape[0]
    slot = (
        lax.broadcasted_iota(jnp.int32, (rows, LANES), 0) * LANES
        + lax.broadcasted_iota(jnp.int32, (rows, LANES), 1)
    )
    first_bin = lax.axis_index("rec") * h_ref.shape[0] * LANES
    raw_ref[0:rows, :] = jnp.where(slot < live_ref[0], animal_ref[...], -1).astype(F32)
    raw_ref[rows : 2 * rows, :] = y_ref[...]
    raw_ref[2 * rows : 3 * rows, :] = (bin_ref[...] - first_bin).astype(F32)
    mine_ref[0 : e_ref.shape[0], :] = e_ref[...]
    mine_ref[e_ref.shape[0] :, :] = h_ref[...]


def prepare(live, animal, y, bins, e, h):
    rows = animal.shape[0]
    return pl.pallas_call(
        prepare_kernel,
        in_specs=[SMEM] + [VMEM] * 5,
        out_specs=[VMEM, VMEM],
        out_shape=[
            jax.ShapeDtypeStruct((3 * rows, LANES), F32),
            jax.ShapeDtypeStruct((e.shape[0] + h.shape[0], LANES), F32),
        ],
        name="prepare",
    )(live, animal, y, bins, e, h)


def up(x, k):
    return jnp.concatenate([x[k:], jnp.zeros((k,) + x.shape[1:], x.dtype)], axis=0)


def down(x, k):
    return jnp.concatenate([jnp.zeros((k,) + x.shape[1:], x.dtype), x[:-k]], axis=0)


def compact(srcs, base, key_s, y_s):
    src_rows = srcs[0].shape[0] // 3
    keys, ys = [], []
    for src in srcs:
        local = src[0:src_rows, :].astype(jnp.int32) - base
        which = src[2 * src_rows : 3 * src_rows, :].astype(jnp.int32)
        known = (local >= 0) & (local < (1 << SPAN_BITS))
        keys.append(jnp.where(known, (which << SPAN_BITS) + local, -1))
        ys.append(src[src_rows : 2 * src_rows, :])
    key = jnp.concatenate(keys, axis=0)
    y = jnp.concatenate(ys, axis=0)
    total = key.shape[0]
    gone = jnp.where(key < 0, 1, 0)
    left = gone
    k = 1
    while k < total:
        left = left + down(left, k)
        k *= 2
    most = total - jnp.min(left[total - 1 : total, :])
    left = left - gone
    k = 1
    while k < total:
        move = (key >= 0) & ((left & k) != 0)
        key_up = up(jnp.where(move, key, -1), k)
        key_up = jnp.concatenate([key_up[: total - k], jnp.full((k, LANES), -1, jnp.int32)], axis=0)
        come = key_up >= 0
        key = jnp.where(come, key_up, jnp.where(move, -1, key))
        y = jnp.where(come, up(y, k), y)
        left = jnp.where(come, up(left, k), left)
        k *= 2
    key_s[...] = key
    y_s[...] = y
    return most


def look_up(t, mine_ref, theirs_ref, first, key_s, y_s, lane_s, sub_s, v_s):
    for g in range(CHUNK_ROWS // 8):
        at = pl.ds(pl.multiple_of(t * CHUNK_ROWS + g * 8, 8), 8)
        key, y = key_s[at, :], y_s[at, :]
        local, which = key & ((1 << SPAN_BITS) - 1), key >> SPAN_BITS
        lane = (local & (LANES - 1)) | ((local >> 13) << 7)
        lane_s[at, :] = jnp.where(key >= 0, lane, -1).astype(F32)
        sub_s[at, :] = ((local >> 7) & (SUBS - 1)).astype(F32)
        low, high = which & (LANES - 1), which >> 7
        for ch, ref in enumerate((mine_ref, theirs_ref)):
            found = jnp.zeros((8, LANES), F32)
            for q in range(ref.shape[0] - first):
                row = jnp.broadcast_to(ref[first + q : first + q + 1, :], (8, LANES))
                got = jnp.take_along_axis(row, low, axis=1, mode="promise_in_bounds")
                found = jnp.where(high == q, got, found)
            value = y - found
            upper = value.astype(BF16).astype(F32)
            v_s[2 * ch, at, :] = upper
            v_s[2 * ch + 1, at, :] = value - upper


def spread(row, count):
    few = jnp.broadcast_to(row, (16, LANES)).astype(BF16)
    return jnp.broadcast_to(few[None], (count // 16, 16, LANES)).reshape(count, LANES)


def one_hots(t, lane_s, sub_s, v_s, lanes_iota, subs_iota):
    a_cols, b_cols = [], []
    one, zero = jnp.ones((), BF16), jnp.zeros((), BF16)
    for i in range(CHUNK_ROWS):
        at = pl.ds(t * CHUNK_ROWS + i, 1)
        a_cols.append(jnp.where(lanes_iota == spread(lane_s[at, :], 2 * LANES), one, zero))
        mask = subs_iota == spread(sub_s[at, :], SUBS)
        pieces = [jnp.where(mask, spread(v_s[p, at, :], SUBS), zero) for p in range(4)]
        pieces.append(jnp.where(mask, one, zero))
        b_cols.append(jnp.concatenate(pieces, axis=0))
    return jnp.concatenate(b_cols, axis=1), jnp.concatenate(a_cols, axis=1)


def front_kernel(n, n_src, mine_any, theirs_any, *refs):
    srcs_any, g_hbm, kept_ref = refs[:n_src], refs[n_src], refs[n_src + 1]
    outs = refs[n_src + 2 : n_src + 2 + n]
    key_s, y_s, lane_s, sub_s, v_s, acc, tab, gain, mine_ref, theirs_ref, src_s, sem, small_sem = refs[
        n_src + 2 + n :
    ]
    srcs = [src_s.at[k] for k in range(n_src)]
    half, markers = kept_ref.shape
    quarter = half // n
    tile = min(TILE, quarter)
    per = quarter // tile
    rows = quarter // LANES
    e_rows = markers // LANES
    chain, rec, ani = lax.axis_index("chain"), lax.axis_index("rec"), lax.axis_index("ani")

    def place(b):
        return pl.multiple_of(
            lax.rem(rec + b // per, n) * quarter + lax.rem(b, per) * tile, tile
        )

    def load(b):
        at = pl.ds(pl.multiple_of(chain * half + place(b), tile), tile)
        return pltpu.make_async_copy(
            g_hbm.at[at, :], kept_ref.at[pl.ds(place(b), tile), :], sem.at[b]
        )

    small = [
        pltpu.make_async_copy(a, b, small_sem.at[k])
        for k, (a, b) in enumerate(
            zip((*srcs_any, mine_any, theirs_any), (*srcs, mine_ref, theirs_ref))
        )
    ]
    for copy in small:
        copy.start()

    @pl.loop(0, n * per)
    def _(b):
        load(b).start()

    for copy in small:
        copy.wait()
    most = compact(srcs, ani * 2 * half + chain * half, key_s, y_s)
    acc[...] = jnp.zeros_like(acc)
    lanes_iota = lax.broadcasted_iota(jnp.int32, (2 * LANES, LANES), 0).astype(F32).astype(BF16)
    subs_iota = lax.broadcasted_iota(jnp.int32, (SUBS, LANES), 0).astype(F32).astype(BF16)

    @pl.loop(0, (most + CHUNK_ROWS - 1) // CHUNK_ROWS)
    def _(t):
        look_up(t, mine_ref, theirs_ref, e_rows, key_s, y_s, lane_s, sub_s, v_s)
        b, a = one_hots(t, lane_s, sub_s, v_s, lanes_iota, subs_iota)
        acc[...] += lax.dot_general(b, a, NT, preferred_element_type=F32)

    for q in range(n):
        wide, first = divmod(q * rows, SUBS)
        cols = slice(wide * LANES, (wide + 1) * LANES)
        window = lambda p: acc[p * SUBS + first : p * SUBS + first + rows, cols]
        tab[0, q] = window(0) + window(1)
        tab[1, q] = window(2) + window(3)
        tab[2, q] = window(4)
    for j in range(n):
        owner = lax.rem(rec + j, n)
        for p in range(3):
            outs[j][(2 + p) * rows : (3 + p) * rows, :] = tab[p, owner]

    e2 = jnp.concatenate(
        [
            jnp.concatenate([ref[i : i + 1, :] for i in range(e_rows)], axis=1)
            for ref in (mine_ref, theirs_ref)
        ]
        + [jnp.zeros((6, markers), F32)],
        axis=0,
    ).astype(BF16)

    @pl.loop(0, n * per)
    def _(b):
        load(b).wait()
        res = lax.dot_general(
            e2, kept_ref[pl.ds(place(b), tile), :], NT, preferred_element_type=F32
        )
        for i in range(tile // LANES):
            at = lax.rem(b, per) * (tile // LANES) + i
            gain[b // per, pl.ds(at, 1), :] = res[0:1, i * LANES : (i + 1) * LANES]
            gain[b // per, pl.ds(rows + at, 1), :] = res[1:2, i * LANES : (i + 1) * LANES]

    for j in range(n):
        outs[j][0 : 2 * rows, :] = gain[j]


def front(genotypes, mine, theirs, srcs, n):
    block, markers = genotypes.shape
    half = block // 2
    total = len(srcs) * srcs[0].shape[0] // 3
    rows = half // n // LANES
    tiles = half // min(TILE, half // n)
    return pl.pallas_call(
        functools.partial(front_kernel, n, len(srcs)),
        in_specs=[ANY] * (3 + len(srcs)),
        out_specs=[VMEM] * (1 + n),
        out_shape=[pltpu.VMEM((half, markers), BF16)]
        + [jax.ShapeDtypeStruct((5 * rows, LANES), F32)] * n,
        scratch_shapes=[
            pltpu.VMEM((total, LANES), jnp.int32),
            pltpu.VMEM((total, LANES), F32),
            pltpu.VMEM((total, LANES), F32),
            pltpu.VMEM((total, LANES), F32),
            pltpu.VMEM((4, total, LANES), F32),
            pltpu.VMEM((5 * SUBS, 2 * LANES), F32),
            pltpu.VMEM((3, n, rows, LANES), F32),
            pltpu.VMEM((n, 2 * rows, LANES), F32),
            pltpu.VMEM(mine.shape, F32),
            pltpu.VMEM(theirs.shape, F32),
            pltpu.VMEM((len(srcs),) + srcs[0].shape, F32),
            pltpu.SemaphoreType.DMA((tiles,)),
            pltpu.SemaphoreType.DMA((2 + len(srcs),)),
        ],
        compiler_params=pltpu.CompilerParams(vmem_limit_bytes=16 << 20),
        cost_estimate=pl.CostEstimate(
            flops=8 * half * markers, bytes_accessed=2 * half * markers, transcendentals=0
        ),
        name="front",
    )(*[pltpu.with_memory_space_constraint(x, pltpu.HBM) for x in (mine, theirs, *srcs)], genotypes)


def pinned(x):
    return pltpu.with_memory_space_constraint(x, pltpu.VMEM)


def combine_kernel(kept_ref, *refs):
    parts, out_ref = refs[:-1], refs[-1]
    rows = out_ref.shape[0] // 2
    total = parts[0][...]
    for part in parts[1:]:
        total = total + part[...]
    count = total[4 * rows :]
    for ch in range(2):
        gain = total[ch * rows : (ch + 1) * rows]
        out_ref[ch * rows : (ch + 1) * rows, :] = (
            total[(2 + ch) * rows : (3 + ch) * rows] - count * gain
        )


def combine(kept, parts):
    rows = parts[0].shape[0] // 5
    return pl.pallas_call(
        combine_kernel,
        in_specs=[VMEM] * (1 + len(parts)),
        out_specs=VMEM,
        out_shape=jax.ShapeDtypeStruct((2 * rows, LANES), F32),
        compiler_params=pltpu.CompilerParams(vmem_limit_bytes=16 << 20),
        cost_estimate=pl.CostEstimate(flops=1 << 16, bytes_accessed=1 << 16, transcendentals=0),
        name="combine",
    )(pinned(kept), *parts)


def product(kept_ref, parts, first, n):
    quarter = kept_ref.shape[0] // n
    rows = quarter // LANES
    rec = lax.axis_index("rec")
    total = jnp.zeros((8, kept_ref.shape[1]), F32)
    for j, part in enumerate(parts):
        cols = [
            jnp.concatenate(
                [part[i : i + 1, :], part[rows + i : rows + i + 1, :], jnp.zeros((6, LANES), F32)],
                axis=0,
            )
            for i in range(rows)
        ]
        lhs = jnp.concatenate(cols, axis=1).astype(BF16)
        at = pl.multiple_of(lax.rem(rec + first + j, n) * quarter, quarter)
        total = total + jnp.dot(
            lhs, kept_ref[pl.ds(at, quarter), :], preferred_element_type=F32
        )
    return total


def back_first_kernel(n, kept_ref, part_ref, out_ref):
    out_ref[...] = product(kept_ref, [part_ref], 0, n)


def back_first(kept, part, n):
    half, markers = kept.shape
    return pl.pallas_call(
        functools.partial(back_first_kernel, n),
        in_specs=[VMEM, VMEM],
        out_specs=VMEM,
        out_shape=jax.ShapeDtypeStruct((8, markers), F32),
        compiler_params=pltpu.CompilerParams(vmem_limit_bytes=16 << 20),
        cost_estimate=pl.CostEstimate(
            flops=4 * half // n * markers, bytes_accessed=2 * half // n * markers, transcendentals=0
        ),
        name="back_first",
    )(pinned(kept), part)


def back_rest_kernel(n, kept_ref, before_ref, *refs):
    parts, (own_ref, other_ref, theirs_ref) = refs[:n], refs[n:]
    rows = parts[0].shape[0] // 2
    for j in range(n):
        theirs_ref[j * rows : (j + 1) * rows, :] = parts[j][rows : 2 * rows, :]
    total = before_ref[...] + product(kept_ref, parts[1:], 1, n)
    for i in range(own_ref.shape[0]):
        own_ref[i : i + 1, :] = total[0:1, i * LANES : (i + 1) * LANES]
        other_ref[i : i + 1, :] = total[1:2, i * LANES : (i + 1) * LANES]


def back_rest(kept, before, parts, n):
    half, markers = kept.shape
    rows = half // n // LANES
    grad = jax.ShapeDtypeStruct((markers // LANES, LANES), F32)
    return pl.pallas_call(
        functools.partial(back_rest_kernel, n),
        in_specs=[VMEM] * (2 + n),
        out_specs=[VMEM] * 3,
        out_shape=[grad, grad, jax.ShapeDtypeStruct((n * rows, LANES), F32)],
        compiler_params=pltpu.CompilerParams(vmem_limit_bytes=16 << 20),
        cost_estimate=pl.CostEstimate(
            flops=4 * half * markers, bytes_accessed=2 * half * markers, transcendentals=0
        ),
        name="back_rest",
    )(pinned(kept), before, *parts)


def assemble_kernel(n, theirs_ref, *refs):
    parts, out_ref = refs[:n], refs[n]
    rows = parts[0].shape[0] // 2
    chain, rec = lax.axis_index("chain"), lax.axis_index("rec")
    for j in range(n):
        owner = lax.rem(rec + j, n)
        out_ref[chain * n + owner] = parts[j][0:rows, :]
        out_ref[(1 - chain) * n + owner] = theirs_ref[j * rows : (j + 1) * rows, :]


def assemble(theirs, parts, n):
    rows = parts[0].shape[0] // 2
    return pl.pallas_call(
        functools.partial(assemble_kernel, n),
        in_specs=[VMEM] * (1 + n),
        out_specs=VMEM,
        out_shape=jax.ShapeDtypeStruct((2 * n, rows, LANES), F32),
        name="assemble",
    )(theirs, *parts)


def on_device(
    n_rec,
    n_ani,
    genotypes,
    effects,
    gaussian_draw,
    prior_prec,
    accept,
    herd_effect,
    phenotype,
    record_animal,
    record_bin,
    live_records,
):
    step_size = 0.005
    rows = genotypes.shape[0] // 2 // n_rec // LANES

    raw, mine = prepare(
        live_records,
        tiled(record_animal),
        tiled(phenotype),
        tiled(record_bin),
        tiled(effects),
        tiled(herd_effect),
    )
    theirs = permute(mine, "chain", 2, 1)
    srcs = [raw] + [permute(raw, "ani", n_ani, k) for k in range(1, n_ani)]

    kept, *sums = front(genotypes, mine, theirs, srcs, n_rec)
    sums = [sums[0]] + [permute(sums[k], "rec", n_rec, k) for k in range(1, n_rec)]
    resid = combine(kept, sums)
    parts = [resid] + [permute(resid, "rec", n_rec, n_rec - k) for k in range(1, n_rec)]
    grads = back_first(kept, resid, n_rec)
    own, other, halves = back_rest(kept, grads, parts, n_rec)
    grad_part = (own + permute(other, "chain", 2, 1)).reshape(-1)
    swapped = permute(halves, "chain", 2, 1)
    resid_sum = assemble(swapped, parts, n_rec).reshape(-1)

    likelihood_grad = jnp.sum(lax.all_gather(grad_part, "ani"), axis=0)
    gradient = likelihood_grad - prior_prec * effects
    proposal = effects + step_size * gradient + math.sqrt(2.0 * step_size) * gaussian_draw
    accepted = jnp.repeat(accept, BLOCK) == 1
    return (jnp.where(accepted, proposal, effects), resid_sum)


def solution(mesh):
    return jax.shard_map(
        functools.partial(on_device, mesh.shape["rec"], mesh.shape["ani"]),
        mesh=mesh,
        in_specs=(
            P("ani", "rec"),
            P(("chain", "rec")),
            P(("chain", "rec")),
            P("rec"),
            P(("chain", "rec")),
            P(("chain", "rec")),
            P(("rec", "ani")),
            P(("rec", "ani")),
            P(("rec", "ani")),
            P(("rec", "ani")),
        ),
        out_specs=(P(("chain", "rec")), P(("chain", "ani"))),
        check_vma=False,
    )
```

```python
import functools
import math

import jax
import jax.numpy as jnp
from jax import lax
from jax.experimental import pallas as pl
from jax.experimental.pallas import tpu as pltpu
from jax.sharding import PartitionSpec as P

BLOCK = 128
LANES = 128
SUBS = 64
SPAN_BITS = 14
CHUNK_ROWS = 16
TILE = 1024
LIMIT = 14 << 20
F32 = jnp.float32
BF16 = jnp.bfloat16
NT = (((1,), (1,)), ((), ()))
VMEM = pl.BlockSpec(memory_space=pltpu.VMEM)
SMEM = pl.BlockSpec(memory_space=pltpu.SMEM)
ANY = pl.BlockSpec(memory_space=pl.ANY)


def swap(x, axis, size, j):
    return lax.ppermute(x, axis, [(i, i ^ j) for i in range(size)])


def tiled(x):
    return x.reshape(-1, LANES)


def prepare_kernel(bins, live_ref, animal_ref, y_ref, bin_ref, raw_ref):
    rows = animal_ref.shape[0]
    slot = (
        lax.broadcasted_iota(jnp.int32, (rows, LANES), 0) * LANES
        + lax.broadcasted_iota(jnp.int32, (rows, LANES), 1)
    )
    first_bin = lax.axis_index("rec") * bins
    raw_ref[0:rows, :] = jnp.where(slot < live_ref[...], animal_ref[...], -1).astype(F32)
    raw_ref[rows : 2 * rows, :] = y_ref[...]
    raw_ref[2 * rows : 3 * rows, :] = (bin_ref[...] - first_bin).astype(F32)


def prepare(bins, live, animal, y, which):
    rows = animal.shape[0]
    return pl.pallas_call(
        functools.partial(prepare_kernel, bins),
        in_specs=[VMEM] * 4,
        out_specs=VMEM,
        out_shape=pltpu.HBM((3 * rows, LANES), F32),
        name="prepare",
    )(live, animal, y, which)


def up(x, k):
    return jnp.concatenate([x[k:], jnp.zeros((k,) + x.shape[1:], x.dtype)], axis=0)


def down(x, k):
    return jnp.concatenate([jnp.zeros((k,) + x.shape[1:], x.dtype), x[:-k]], axis=0)


def compact(srcs, base, key_s, y_s):
    src_rows = srcs[0].shape[0] // 3
    keys, ys = [], []
    for src in srcs:
        local = src[0:src_rows, :].astype(jnp.int32) - base
        which = src[2 * src_rows : 3 * src_rows, :].astype(jnp.int32)
        known = (local >= 0) & (local < (1 << SPAN_BITS))
        keys.append(jnp.where(known, (which << SPAN_BITS) + local, -1))
        ys.append(src[src_rows : 2 * src_rows, :])
    key = jnp.concatenate(keys, axis=0)
    y = jnp.concatenate(ys, axis=0)
    total = key.shape[0]
    gone = jnp.where(key < 0, 1, 0)
    left = gone
    k = 1
    while k < total:
        left = left + down(left, k)
        k *= 2
    most = total - jnp.min(left[total - 1 : total, :])
    left = left - gone
    k = 1
    while k < total:
        move = (key >= 0) & ((left & k) != 0)
        key_up = up(jnp.where(move, key, -1), k)
        key_up = jnp.concatenate([key_up[: total - k], jnp.full((k, LANES), -1, jnp.int32)], axis=0)
        come = key_up >= 0
        key = jnp.where(come, key_up, jnp.where(move, -1, key))
        y = jnp.where(come, up(y, k), y)
        left = jnp.where(come, up(left, k), left)
        k *= 2
    key_s[...] = key
    y_s[...] = y
    return most


def look_up(t, herds, key_s, y_s, lane_s, sub_s, v_s):
    for g in range(CHUNK_ROWS // 8):
        at = pl.ds(pl.multiple_of(t * CHUNK_ROWS + g * 8, 8), 8)
        key, y = key_s[at, :], y_s[at, :]
        local, which = key & ((1 << SPAN_BITS) - 1), key >> SPAN_BITS
        lane = (local & (LANES - 1)) | ((local >> 13) << 7)
        lane_s[at, :] = jnp.where(key >= 0, lane, -1).astype(F32)
        sub_s[at, :] = ((local >> 7) & (SUBS - 1)).astype(F32)
        low, high = which & (LANES - 1), which >> 7
        for ch, ref in enumerate(herds):
            found = jnp.zeros((8, LANES), F32)
            for q in range(ref.shape[0]):
                row = jnp.broadcast_to(ref[q : q + 1, :], (8, LANES))
                got = jnp.take_along_axis(row, low, axis=1, mode="promise_in_bounds")
                found = jnp.where(high == q, got, found)
            value = y - found
            upper = value.astype(BF16).astype(F32)
            v_s[2 * ch, at, :] = upper
            v_s[2 * ch + 1, at, :] = value - upper


def spread(row, count):
    few = jnp.broadcast_to(row, (16, LANES)).astype(BF16)
    return jnp.broadcast_to(few[None], (count // 16, 16, LANES)).reshape(count, LANES)


def one_hots(t, lane_s, sub_s, v_s, lanes_iota, subs_iota):
    a_cols, b_cols = [], []
    one, zero = jnp.ones((), BF16), jnp.zeros((), BF16)
    for i in range(CHUNK_ROWS):
        at = pl.ds(t * CHUNK_ROWS + i, 1)
        a_cols.append(jnp.where(lanes_iota == spread(lane_s[at, :], 2 * LANES), one, zero))
        mask = subs_iota == spread(sub_s[at, :], SUBS)
        pieces = [jnp.where(mask, spread(v_s[p, at, :], SUBS), zero) for p in range(4)]
        pieces.append(jnp.where(mask, one, zero))
        b_cols.append(jnp.concatenate(pieces, axis=0))
    return jnp.concatenate(b_cols, axis=1), jnp.concatenate(a_cols, axis=1)


def gains(e2, kept_ref, at, count, out_ref, row, rows):
    res = lax.dot_general(e2, kept_ref[pl.ds(at, count), :], NT, preferred_element_type=F32)
    for i in range(count // LANES):
        for ch in range(2):
            out_ref[pl.ds(ch * rows + row + i, 1), :] = res[
                ch : ch + 1, i * LANES : (i + 1) * LANES
            ]


def front_a_kernel(n, own_any, other_any, g_hbm, kept_ref, gains_any, gain, own_s, other_s, sem, small_sem, out_sem):
    markers = kept_ref.shape[1]
    quarter = (kept_ref.shape[0] - 16) // (n // 2)
    chain, rec = lax.axis_index("chain"), lax.axis_index("rec")
    small = [
        pltpu.make_async_copy(a, b, small_sem.at[k])
        for k, (a, b) in enumerate([(own_any, own_s), (other_any, other_s)])
    ]
    for copy in small:
        copy.start()
    tile = min(TILE, quarter)
    per = quarter // tile
    rows = quarter // LANES

    def load(b):
        at = chain * quarter * n + (rec ^ (b // per)) * quarter + lax.rem(b, per) * tile
        return pltpu.make_async_copy(
            g_hbm.at[pl.ds(pl.multiple_of(at, tile), tile), :],
            kept_ref.at[pl.ds(pl.multiple_of(b * tile, tile), tile), :],
            sem.at[b],
        )

    @pl.loop(0, n // 2 * per)
    def _(b):
        load(b).start()

    for copy in small:
        copy.wait()
    e2 = jnp.concatenate(
        [
            jnp.concatenate([ref[i : i + 1, :] for i in range(markers // LANES)], axis=1)
            for ref in (own_s, other_s)
        ]
        + [jnp.zeros((14, markers), F32)],
        axis=0,
    ).astype(BF16)
    kept_ref[(n // 2) * quarter :, :] = e2

    @pl.loop(0, n // 2 * per)
    def _(b):
        load(b).wait()
        at = pl.multiple_of(b * tile, tile)
        gains(e2[:8], kept_ref, at, tile, gain.at[b // per], lax.rem(b, per) * (tile // LANES), rows)

    done = pltpu.make_async_copy(gain, gains_any, out_sem)
    done.start()
    done.wait()


def front_a(genotypes, effects, n):
    block, markers = genotypes.shape
    half = block // 2
    quarter = half // n
    rows = quarter // LANES
    tiles = n // 2 * (quarter // min(TILE, quarter))
    shape = (n // 2, 2 * rows, LANES)
    return pl.pallas_call(
        functools.partial(front_a_kernel, n),
        in_specs=[ANY] * 3,
        out_specs=[VMEM, ANY],
        out_shape=[pltpu.VMEM((n // 2 * quarter + 16, markers), BF16), pltpu.HBM(shape, F32)],
        scratch_shapes=[
            pltpu.VMEM(shape, F32),
            pltpu.VMEM(effects[0].shape, F32),
            pltpu.VMEM(effects[1].shape, F32),
            pltpu.SemaphoreType.DMA((tiles,)),
            pltpu.SemaphoreType.DMA((2,)),
            pltpu.SemaphoreType.DMA,
        ],
        compiler_params=pltpu.CompilerParams(vmem_limit_bytes=LIMIT),
        cost_estimate=pl.CostEstimate(
            flops=2 * half * markers, bytes_accessed=half * markers, transcendentals=0
        ),
        name="front_a",
    )(*[pltpu.with_memory_space_constraint(x, pltpu.HBM) for x in effects], genotypes)


def front_b_kernel(n, n_src, kept_a_ref, *refs):
    small_any, g_hbm, kept_ref = refs[: n_src + 3], refs[n_src + 3], refs[n_src + 4]
    outs = refs[n_src + 5 : n_src + 5 + n]
    key_s, y_s, lane_s, sub_s, v_s, acc, tab, *small_s, sem, small_sem = refs[n_src + 5 + n :]
    quarter = kept_ref.shape[0] // (n // 2)
    half = quarter * n
    rows = quarter // LANES
    chain, rec, ani = lax.axis_index("chain"), lax.axis_index("rec"), lax.axis_index("ani")

    small = [
        pltpu.make_async_copy(a, b, small_sem.at[k])
        for k, (a, b) in enumerate(zip(small_any, small_s))
    ]
    for copy in small:
        copy.start()
    big = []
    for slot in range(n // 2):
        at = pl.multiple_of(chain * half + (rec ^ (n // 2 + slot)) * quarter, quarter)
        big.append(
            pltpu.make_async_copy(
                g_hbm.at[pl.ds(at, quarter), :],
                kept_ref.at[slot * quarter : (slot + 1) * quarter, :],
                sem.at[slot],
            )
        )
        big[-1].start()
    for copy in small:
        copy.wait()
    srcs, (*herds, gain_a) = small_s[:n_src], small_s[n_src:]

    most = compact(srcs, ani * 2 * half + chain * half, key_s, y_s)
    acc[...] = jnp.zeros_like(acc)
    lanes_iota = lax.broadcasted_iota(jnp.int32, (2 * LANES, LANES), 0).astype(F32).astype(BF16)
    subs_iota = lax.broadcasted_iota(jnp.int32, (SUBS, LANES), 0).astype(F32).astype(BF16)

    @pl.loop(0, (most + CHUNK_ROWS - 1) // CHUNK_ROWS)
    def _(t):
        look_up(t, herds, key_s, y_s, lane_s, sub_s, v_s)
        b, a = one_hots(t, lane_s, sub_s, v_s, lanes_iota, subs_iota)
        acc[...] += lax.dot_general(b, a, NT, preferred_element_type=F32)

    for q in range(n):
        wide, first = divmod(q * rows, SUBS)
        cols = slice(wide * LANES, (wide + 1) * LANES)
        window = lambda p: acc[p * SUBS + first : p * SUBS + first + rows, cols]
        tab[q, 0:rows, :] = window(0) + window(1)
        tab[q, rows : 2 * rows, :] = window(2) + window(3)
        tab[q, 2 * rows : 3 * rows, :] = window(4)
    for j in range(n):
        outs[j][2 * rows : 5 * rows, :] = tab[rec ^ j]
    for j in range(n // 2):
        outs[j][0 : 2 * rows, :] = gain_a[j]
    e2 = kept_a_ref[n // 2 * quarter : n // 2 * quarter + 8, :]
    for slot in range(n // 2):
        big[slot].wait()
        gains(e2, kept_ref, slot * quarter, quarter, outs[n // 2 + slot], 0, rows)


def front_b(genotypes, kept_a, gain_a, herds, srcs, n):
    block, markers = genotypes.shape
    half = block // 2
    quarter = half // n
    total = len(srcs) * srcs[0].shape[0] // 3
    rows = quarter // LANES
    small = [*srcs, *herds, gain_a]
    return pl.pallas_call(
        functools.partial(front_b_kernel, n, len(srcs)),
        in_specs=[VMEM] + [ANY] * (1 + len(small)),
        out_specs=[VMEM] * (1 + n),
        out_shape=[pltpu.VMEM((n // 2 * quarter, markers), BF16)]
        + [jax.ShapeDtypeStruct((5 * rows, LANES), F32)] * n,
        scratch_shapes=[
            pltpu.VMEM((total, LANES), jnp.int32),
            pltpu.VMEM((total, LANES), F32),
            pltpu.VMEM((total, LANES), F32),
            pltpu.VMEM((total, LANES), F32),
            pltpu.VMEM((4, total, LANES), F32),
            pltpu.VMEM((5 * SUBS, 2 * LANES), F32),
            pltpu.VMEM((n, 3 * rows, LANES), F32),
        ]
        + [pltpu.VMEM(x.shape, F32) for x in small]
        + [pltpu.SemaphoreType.DMA((n // 2,)), pltpu.SemaphoreType.DMA((len(small),))],
        compiler_params=pltpu.CompilerParams(vmem_limit_bytes=LIMIT),
        cost_estimate=pl.CostEstimate(
            flops=4 * half * markers, bytes_accessed=half * markers, transcendentals=0
        ),
        name="front_b",
    )(
        pinned(kept_a),
        *[pltpu.with_memory_space_constraint(x, pltpu.HBM) for x in small],
        genotypes,
    )


def pinned(x):
    return pltpu.with_memory_space_constraint(x, pltpu.VMEM)


def combine_kernel(kept_a_ref, kept_b_ref, *refs):
    parts, out_ref = refs[:-1], refs[-1]
    rows = out_ref.shape[0] // 2
    total = parts[0][...]
    for part in parts[1:]:
        total = total + part[...]
    count = total[4 * rows :]
    for ch in range(2):
        gain = total[ch * rows : (ch + 1) * rows]
        out_ref[ch * rows : (ch + 1) * rows, :] = (
            total[(2 + ch) * rows : (3 + ch) * rows] - count * gain
        )


def combine(kept, parts):
    rows = parts[0].shape[0] // 5
    return pl.pallas_call(
        combine_kernel,
        in_specs=[VMEM] * (2 + len(parts)),
        out_specs=VMEM,
        out_shape=jax.ShapeDtypeStruct((2 * rows, LANES), F32),
        compiler_params=pltpu.CompilerParams(vmem_limit_bytes=LIMIT),
        cost_estimate=pl.CostEstimate(flops=1 << 16, bytes_accessed=1 << 16, transcendentals=0),
        name="combine",
    )(*map(pinned, kept), *parts)


def product(n, kept_refs, js, parts):
    quarter = kept_refs[1].shape[0] // (n // 2)
    rows = quarter // LANES
    total = jnp.zeros((8, kept_refs[1].shape[1]), F32)
    for j, part in zip(js, parts):
        cols = [
            jnp.concatenate(
                [part[i : i + 1, :], part[rows + i : rows + i + 1, :], jnp.zeros((6, LANES), F32)],
                axis=0,
            )
            for i in range(rows)
        ]
        lhs = jnp.concatenate(cols, axis=1).astype(BF16)
        late, slot = divmod(j, n // 2)
        total = total + jnp.dot(
            lhs,
            kept_refs[late][slot * quarter : (slot + 1) * quarter, :],
            preferred_element_type=F32,
        )
    return total


def back_kernel(n, js, kept_a_ref, kept_b_ref, *refs):
    parts, before, out_ref = refs[: len(js)], refs[len(js) : -1], refs[-1]
    total = product(n, (kept_a_ref, kept_b_ref), js, parts)
    out_ref[...] = total + before[0][...] if before else total


def back(kept, js, parts, n, *before):
    quarter, markers = kept[1].shape[0] // (n // 2), kept[1].shape[1]
    return pl.pallas_call(
        functools.partial(back_kernel, n, js),
        in_specs=[VMEM] * (2 + len(js) + len(before)),
        out_specs=VMEM,
        out_shape=jax.ShapeDtypeStruct((8, markers), F32),
        compiler_params=pltpu.CompilerParams(vmem_limit_bytes=LIMIT),
        cost_estimate=pl.CostEstimate(
            flops=4 * quarter * markers * len(js),
            bytes_accessed=2 * quarter * markers * len(js),
            transcendentals=0,
        ),
        name="back",
    )(*map(pinned, kept), *parts, *before)


def back_last_kernel(n, js, kept_a_ref, kept_b_ref, before_ref, *refs):
    parts, (own_ref, other_ref, theirs_ref) = refs[:n], refs[n:]
    rows = parts[0].shape[0] // 2
    for j in range(n):
        theirs_ref[j * rows : (j + 1) * rows, :] = parts[j][rows : 2 * rows, :]
    total = before_ref[...] + product(n, (kept_a_ref, kept_b_ref), js, [parts[j] for j in js])
    for i in range(own_ref.shape[0]):
        own_ref[i : i + 1, :] = total[0:1, i * LANES : (i + 1) * LANES]
        other_ref[i : i + 1, :] = total[1:2, i * LANES : (i + 1) * LANES]


def back_last(kept, js, parts, n, before):
    quarter, markers = kept[1].shape[0] // (n // 2), kept[1].shape[1]
    grad = jax.ShapeDtypeStruct((markers // LANES, LANES), F32)
    return pl.pallas_call(
        functools.partial(back_last_kernel, n, js),
        in_specs=[VMEM] * (3 + n),
        out_specs=[VMEM] * 3,
        out_shape=[grad, grad, jax.ShapeDtypeStruct((n * quarter // LANES, LANES), F32)],
        compiler_params=pltpu.CompilerParams(vmem_limit_bytes=LIMIT),
        cost_estimate=pl.CostEstimate(
            flops=4 * quarter * markers * len(js),
            bytes_accessed=2 * quarter * markers * len(js),
            transcendentals=0,
        ),
        name="back_last",
    )(*map(pinned, kept), before, *parts)


def assemble_kernel(n, theirs_ref, *refs):
    parts, out_ref = refs[:n], refs[n]
    rows = parts[0].shape[0] // 2
    chain, rec = lax.axis_index("chain"), lax.axis_index("rec")
    for j in range(n):
        owner = rec ^ j
        out_ref[chain * n + owner] = parts[j][0:rows, :]
        out_ref[(1 - chain) * n + owner] = theirs_ref[j * rows : (j + 1) * rows, :]


def assemble(theirs, parts, n):
    rows = parts[0].shape[0] // 2
    return pl.pallas_call(
        functools.partial(assemble_kernel, n),
        in_specs=[VMEM] * (1 + n),
        out_specs=VMEM,
        out_shape=jax.ShapeDtypeStruct((2 * n, rows, LANES), F32),
        cost_estimate=pl.CostEstimate(flops=1 << 16, bytes_accessed=1 << 18, transcendentals=0),
        name="assemble",
    )(theirs, *parts)


def on_device(
    n_rec,
    n_ani,
    genotypes,
    effects,
    gaussian_draw,
    prior_prec,
    accept,
    herd_effect,
    phenotype,
    record_animal,
    record_bin,
    live_records,
):
    step_size = 0.005
    n = n_rec

    effects_2d, herd_2d = tiled(effects), tiled(herd_effect)
    theirs = (swap(effects_2d, "chain", 2, 1), swap(herd_2d, "chain", 2, 1))
    raw = prepare(
        herd_effect.shape[0],
        live_records.reshape(1, 1),
        tiled(record_animal),
        tiled(phenotype),
        tiled(record_bin),
    )
    theirs, raw = lax.optimization_barrier((theirs, raw))
    srcs = [raw] + [swap(raw, "ani", n_ani, j) for j in range(1, n_ani)]

    kept_a, gain_a = front_a(genotypes, [effects_2d, theirs[0]], n)
    kept_b, *sums = front_b(genotypes, kept_a, gain_a, [herd_2d, theirs[1]], srcs, n)
    kept = (kept_a, kept_b)
    resid = combine(kept, [sums[0]] + [swap(sums[j], "rec", n, j) for j in range(1, n)])

    parts = [resid] + [swap(resid, "rec", n, j) for j in range(1, n)]
    grads = back(kept, [0], [resid], n)
    steps = [list(range(j, min(j + n // 4, n))) for j in range(1, n, n // 4)]
    for js in steps[:-1]:
        grads = back(kept, js, [parts[j] for j in js], n, grads)
    own, other, halves = back_last(kept, steps[-1], parts, n, grads)
    grad_part = own + swap(other, "chain", 2, 1)
    grad_part, swapped = lax.optimization_barrier((grad_part, swap(halves, "chain", 2, 1)))
    resid_sum = assemble(swapped, parts, n).reshape(-1)
    others = [swap(grad_part, "ani", n_ani, j) for j in range(1, n_ani)]

    likelihood_grad = grad_part
    for x in others:
        likelihood_grad = likelihood_grad + x
    likelihood_grad = likelihood_grad.reshape(-1)
    gradient = likelihood_grad - prior_prec * effects
    proposal = effects + step_size * gradient + math.sqrt(2.0 * step_size) * gaussian_draw
    accepted = jnp.repeat(accept, BLOCK) == 1
    return (jnp.where(accepted, proposal, effects), resid_sum)


def solution(mesh):
    return jax.shard_map(
        functools.partial(on_device, mesh.shape["rec"], mesh.shape["ani"]),
        mesh=mesh,
        in_specs=(
            P("ani", "rec"),
            P(("chain", "rec")),
            P(("chain", "rec")),
            P("rec"),
            P(("chain", "rec")),
            P(("chain", "rec")),
            P(("rec", "ani")),
            P(("rec", "ani")),
            P(("rec", "ani")),
            P(("rec", "ani")),
        ),
        out_specs=(P(("chain", "rec")), P(("chain", "ani"))),
        check_vma=False,
    )
```

```python
import functools
import math

import jax
import jax.numpy as jnp
from jax import lax
from jax.experimental import pallas as pl
from jax.experimental.pallas import tpu as pltpu
from jax.sharding import PartitionSpec as P

BLOCK = 128
LANES = 128
SUBS = 64
SPAN_BITS = 14
CHUNK_ROWS = 16
TILE = 1024
LIMIT = 14 << 20
F32 = jnp.float32
BF16 = jnp.bfloat16
NT = (((1,), (1,)), ((), ()))
VMEM = pl.BlockSpec(memory_space=pltpu.VMEM)
SMEM = pl.BlockSpec(memory_space=pltpu.SMEM)
ANY = pl.BlockSpec(memory_space=pl.ANY)


def swap(x, axis, size, j):
    return lax.ppermute(x, axis, [(i, i ^ j) for i in range(size)])


def shift(x, axis, size, j):
    return lax.ppermute(x, axis, [(i, (i + j) % size) for i in range(size)])


def tiled(x):
    return x.reshape(-1, LANES)


def prepare_kernel(bins, live_ref, animal_ref, y_ref, bin_ref, raw_ref):
    rows = animal_ref.shape[0]
    slot = (
        lax.broadcasted_iota(jnp.int32, (rows, LANES), 0) * LANES
        + lax.broadcasted_iota(jnp.int32, (rows, LANES), 1)
    )
    first_bin = lax.axis_index("rec") * bins
    raw_ref[0:rows, :] = jnp.where(slot < live_ref[...], animal_ref[...], -1).astype(F32)
    raw_ref[rows : 2 * rows, :] = y_ref[...]
    raw_ref[2 * rows : 3 * rows, :] = (bin_ref[...] - first_bin).astype(F32)


def prepare(bins, live, animal, y, which):
    rows = animal.shape[0]
    return pl.pallas_call(
        functools.partial(prepare_kernel, bins),
        in_specs=[VMEM] * 4,
        out_specs=VMEM,
        out_shape=pltpu.HBM((3 * rows, LANES), F32),
        name="prepare",
    )(live, animal, y, which)


def up(x, k):
    return jnp.concatenate([x[k:], jnp.zeros((k,) + x.shape[1:], x.dtype)], axis=0)


def down(x, k):
    return jnp.concatenate([jnp.zeros((k,) + x.shape[1:], x.dtype), x[:-k]], axis=0)


def compact(srcs, base, key_s, y_s):
    src_rows = srcs[0].shape[0] // 3
    keys, ys = [], []
    for src in srcs:
        local = src[0:src_rows, :].astype(jnp.int32) - base
        which = src[2 * src_rows : 3 * src_rows, :].astype(jnp.int32)
        known = (local >= 0) & (local < (1 << SPAN_BITS))
        keys.append(jnp.where(known, (which << SPAN_BITS) + local, -1))
        ys.append(src[src_rows : 2 * src_rows, :])
    key = jnp.concatenate(keys, axis=0)
    y = jnp.concatenate(ys, axis=0)
    total = key.shape[0]
    gone = jnp.where(key < 0, 1, 0)
    left = gone
    k = 1
    while k < total:
        left = left + down(left, k)
        k *= 2
    most = total - jnp.min(left[total - 1 : total, :])
    left = left - gone
    k = 1
    while k < total:
        move = (key >= 0) & ((left & k) != 0)
        key_up = up(jnp.where(move, key, -1), k)
        key_up = jnp.concatenate([key_up[: total - k], jnp.full((k, LANES), -1, jnp.int32)], axis=0)
        come = key_up >= 0
        key = jnp.where(come, key_up, jnp.where(move, -1, key))
        y = jnp.where(come, up(y, k), y)
        left = jnp.where(come, up(left, k), left)
        k *= 2
    key_s[...] = key
    y_s[...] = y
    return most


def look_up(t, herds, key_s, y_s, lane_s, sub_s, v_s):
    for g in range(CHUNK_ROWS // 8):
        at = pl.ds(pl.multiple_of(t * CHUNK_ROWS + g * 8, 8), 8)
        key, y = key_s[at, :], y_s[at, :]
        local, which = key & ((1 << SPAN_BITS) - 1), key >> SPAN_BITS
        lane = (local & (LANES - 1)) | ((local >> 13) << 7)
        lane_s[at, :] = jnp.where(key >= 0, lane, -1).astype(F32)
        sub_s[at, :] = ((local >> 7) & (SUBS - 1)).astype(F32)
        low, high = which & (LANES - 1), which >> 7
        for ch, ref in enumerate(herds):
            found = jnp.zeros((8, LANES), F32)
            for q in range(ref.shape[0]):
                row = jnp.broadcast_to(ref[q : q + 1, :], (8, LANES))
                got = jnp.take_along_axis(row, low, axis=1, mode="promise_in_bounds")
                found = jnp.where(high == q, got, found)
            value = y - found
            upper = value.astype(BF16).astype(F32)
            v_s[2 * ch, at, :] = upper
            v_s[2 * ch + 1, at, :] = value - upper


def spread(row, count):
    few = jnp.broadcast_to(row, (16, LANES)).astype(BF16)
    return jnp.broadcast_to(few[None], (count // 16, 16, LANES)).reshape(count, LANES)


def one_hots(t, lane_s, sub_s, v_s, lanes_iota, subs_iota):
    a_cols, b_cols = [], []
    one, zero = jnp.ones((), BF16), jnp.zeros((), BF16)
    for i in range(CHUNK_ROWS):
        at = pl.ds(t * CHUNK_ROWS + i, 1)
        a_cols.append(jnp.where(lanes_iota == spread(lane_s[at, :], 2 * LANES), one, zero))
        mask = subs_iota == spread(sub_s[at, :], SUBS)
        pieces = [jnp.where(mask, spread(v_s[p, at, :], SUBS), zero) for p in range(4)]
        pieces.append(jnp.where(mask, one, zero))
        b_cols.append(jnp.concatenate(pieces, axis=0))
    return jnp.concatenate(b_cols, axis=1), jnp.concatenate(a_cols, axis=1)


def gains(e2, kept_ref, at, count, out_ref, row, rows):
    res = lax.dot_general(e2, kept_ref[pl.ds(at, count), :], NT, preferred_element_type=F32)
    for i in range(count // LANES):
        for ch in range(2):
            out_ref[pl.ds(ch * rows + row + i, 1), :] = res[
                ch : ch + 1, i * LANES : (i + 1) * LANES
            ]


def front_a_kernel(n, own_any, other_any, g_hbm, kept_ref, gains_any, gain, own_s, other_s, sem, small_sem, out_sem):
    markers = kept_ref.shape[1]
    quarter = (kept_ref.shape[0] - 16) // (n // 2)
    chain, rec = lax.axis_index("chain"), lax.axis_index("rec")
    small = [
        pltpu.make_async_copy(a, b, small_sem.at[k])
        for k, (a, b) in enumerate([(own_any, own_s), (other_any, other_s)])
    ]
    for copy in small:
        copy.start()
    tile = min(TILE, quarter)
    per = quarter // tile
    rows = quarter // LANES

    def load(b):
        owner = rec ^ (2 * (b // per) + 1)
        at = chain * quarter * n + owner * quarter + lax.rem(b, per) * tile
        return pltpu.make_async_copy(
            g_hbm.at[pl.ds(pl.multiple_of(at, tile), tile), :],
            kept_ref.at[pl.ds(pl.multiple_of(b * tile, tile), tile), :],
            sem.at[b],
        )

    @pl.loop(0, n // 2 * per)
    def _(b):
        load(b).start()

    for copy in small:
        copy.wait()
    e2 = jnp.concatenate(
        [
            jnp.concatenate([ref[i : i + 1, :] for i in range(markers // LANES)], axis=1)
            for ref in (own_s, other_s)
        ]
        + [jnp.zeros((14, markers), F32)],
        axis=0,
    ).astype(BF16)
    kept_ref[(n // 2) * quarter :, :] = e2

    @pl.loop(0, n // 4 * per)
    def _(b):
        load(b).wait()
        at = pl.multiple_of(b * tile, tile)
        gains(e2[:8], kept_ref, at, tile, gain.at[b // per], lax.rem(b, per) * (tile // LANES), rows)

    done = pltpu.make_async_copy(gain, gains_any, out_sem)
    done.start()

    @pl.loop(n // 4 * per, n // 2 * per)
    def _(b):
        load(b).wait()

    done.wait()


def front_a(genotypes, effects, n):
    block, markers = genotypes.shape
    half = block // 2
    quarter = half // n
    rows = quarter // LANES
    tiles = n // 2 * (quarter // min(TILE, quarter))
    shape = (n // 4, 2 * rows, LANES)
    return pl.pallas_call(
        functools.partial(front_a_kernel, n),
        in_specs=[ANY] * 3,
        out_specs=[VMEM, ANY],
        out_shape=[pltpu.VMEM((n // 2 * quarter + 16, markers), BF16), pltpu.HBM(shape, F32)],
        scratch_shapes=[
            pltpu.VMEM(shape, F32),
            pltpu.VMEM(effects[0].shape, F32),
            pltpu.VMEM(effects[1].shape, F32),
            pltpu.SemaphoreType.DMA((tiles,)),
            pltpu.SemaphoreType.DMA((2,)),
            pltpu.SemaphoreType.DMA,
        ],
        compiler_params=pltpu.CompilerParams(vmem_limit_bytes=LIMIT),
        cost_estimate=pl.CostEstimate(
            flops=2 * half * markers, bytes_accessed=half * markers, transcendentals=0
        ),
        name="front_a",
    )(*[pltpu.with_memory_space_constraint(x, pltpu.HBM) for x in effects], genotypes)


def front_b_kernel(n, n_src, kept_a_ref, *refs):
    small_any, g_hbm = refs[: n_src + 3], refs[n_src + 3]
    kept_ref, odd, rest = refs[n_src + 4 : n_src + 7]
    key_s, y_s, lane_s, sub_s, v_s, acc, tab, *small_s, sem, small_sem = refs[n_src + 7 :]
    quarter = kept_ref.shape[0] // (n // 2)
    half = quarter * n
    rows = quarter // LANES
    chain, rec, ani = lax.axis_index("chain"), lax.axis_index("rec"), lax.axis_index("ani")

    small = [
        pltpu.make_async_copy(a, b, small_sem.at[k])
        for k, (a, b) in enumerate(zip(small_any, small_s))
    ]
    for copy in small:
        copy.start()
    big = []
    for slot in range(n // 2):
        at = pl.multiple_of(chain * half + (rec ^ (2 * slot)) * quarter, quarter)
        big.append(
            pltpu.make_async_copy(
                g_hbm.at[pl.ds(at, quarter), :],
                kept_ref.at[slot * quarter : (slot + 1) * quarter, :],
                sem.at[slot],
            )
        )
        big[-1].start()
    for copy in small:
        copy.wait()
    srcs, (*herds, gain_a) = small_s[:n_src], small_s[n_src:]

    most = compact(srcs, ani * 2 * half + chain * half, key_s, y_s)
    acc[...] = jnp.zeros_like(acc)
    lanes_iota = lax.broadcasted_iota(jnp.int32, (2 * LANES, LANES), 0).astype(F32).astype(BF16)
    subs_iota = lax.broadcasted_iota(jnp.int32, (SUBS, LANES), 0).astype(F32).astype(BF16)

    @pl.loop(0, (most + CHUNK_ROWS - 1) // CHUNK_ROWS)
    def _(t):
        look_up(t, herds, key_s, y_s, lane_s, sub_s, v_s)
        b, a = one_hots(t, lane_s, sub_s, v_s, lanes_iota, subs_iota)
        acc[...] += lax.dot_general(b, a, NT, preferred_element_type=F32)

    for q in range(n):
        wide, first = divmod(q * rows, SUBS)
        cols = slice(wide * LANES, (wide + 1) * LANES)
        window = lambda p: acc[p * SUBS + first : p * SUBS + first + rows, cols]
        tab[q, 0:rows, :] = window(0) + window(1)
        tab[q, rows : 2 * rows, :] = window(2) + window(3)
        tab[q, 2 * rows : 3 * rows, :] = window(4)
    for i in range(n // 2):
        rest[i] = tab[rec ^ (2 * i)]
        odd[i, 2 * rows : 5 * rows, :] = tab[rec ^ (2 * i + 1)]
    for i in range(n // 4):
        odd[i, 0 : 2 * rows, :] = gain_a[i]
    e2 = kept_a_ref[n // 2 * quarter : n // 2 * quarter + 8, :]
    for i in range(n // 4, n // 2):
        gains(e2, kept_a_ref, i * quarter, quarter, odd.at[i], 0, rows)
    for copy in big:
        copy.wait()


def front_b(genotypes, kept_a, gain_a, herds, srcs, n):
    block, markers = genotypes.shape
    half = block // 2
    quarter = half // n
    total = len(srcs) * srcs[0].shape[0] // 3
    rows = quarter // LANES
    small = [*srcs, *herds, gain_a]
    return pl.pallas_call(
        functools.partial(front_b_kernel, n, len(srcs)),
        in_specs=[VMEM] + [ANY] * (1 + len(small)),
        out_specs=[VMEM] * 3,
        out_shape=[
            pltpu.VMEM((n // 2 * quarter, markers), BF16),
            jax.ShapeDtypeStruct((n // 2, 5 * rows, LANES), F32),
            jax.ShapeDtypeStruct((n // 2, 3 * rows, LANES), F32),
        ],
        scratch_shapes=[
            pltpu.VMEM((total, LANES), jnp.int32),
            pltpu.VMEM((total, LANES), F32),
            pltpu.VMEM((total, LANES), F32),
            pltpu.VMEM((total, LANES), F32),
            pltpu.VMEM((4, total, LANES), F32),
            pltpu.VMEM((5 * SUBS, 2 * LANES), F32),
            pltpu.VMEM((n, 3 * rows, LANES), F32),
        ]
        + [pltpu.VMEM(x.shape, F32) for x in small]
        + [pltpu.SemaphoreType.DMA((n // 2,)), pltpu.SemaphoreType.DMA((len(small),))],
        compiler_params=pltpu.CompilerParams(vmem_limit_bytes=LIMIT),
        cost_estimate=pl.CostEstimate(
            flops=4 * half * markers, bytes_accessed=half * markers, transcendentals=0
        ),
        name="front_b",
    )(
        pinned(kept_a),
        *[pltpu.with_memory_space_constraint(x, pltpu.HBM) for x in small],
        genotypes,
    )


def pinned(x):
    return pltpu.with_memory_space_constraint(x, pltpu.VMEM)


def front_c_kernel(n, kept_a_ref, kept_b_ref, rest_ref, *outs):
    quarter = kept_b_ref.shape[0] // (n // 2)
    rows = quarter // LANES
    e2 = kept_a_ref[n // 2 * quarter : n // 2 * quarter + 8, :]
    for i in range(n // 2):
        outs[i][2 * rows : 5 * rows, :] = rest_ref[i]
        gains(e2, kept_b_ref, i * quarter, quarter, outs[i], 0, rows)


def front_c(kept, rest, n):
    quarter, markers = kept[1].shape[0] // (n // 2), kept[1].shape[1]
    piece = jax.ShapeDtypeStruct((5 * quarter // LANES, LANES), F32)
    return pl.pallas_call(
        functools.partial(front_c_kernel, n),
        in_specs=[VMEM] * 3,
        out_specs=[VMEM] * (n // 2),
        out_shape=[piece] * (n // 2),
        compiler_params=pltpu.CompilerParams(vmem_limit_bytes=LIMIT),
        cost_estimate=pl.CostEstimate(
            flops=2 * n * quarter * markers, bytes_accessed=n * quarter * markers, transcendentals=0
        ),
        name="front_c",
    )(*map(pinned, kept), rest)


def merge_kernel(kept_a_ref, kept_b_ref, came_ref, *refs):
    count = len(refs) // 2
    for i in range(count):
        refs[count + i][...] = refs[i][...] + came_ref[i + 1]


def merge(kept, came, pieces):
    return pl.pallas_call(
        merge_kernel,
        in_specs=[VMEM] * (3 + len(pieces)),
        out_specs=[VMEM] * len(pieces),
        out_shape=[jax.ShapeDtypeStruct(x.shape, F32) for x in pieces],
        compiler_params=pltpu.CompilerParams(vmem_limit_bytes=LIMIT),
        cost_estimate=pl.CostEstimate(flops=1 << 16, bytes_accessed=1 << 16, transcendentals=0),
        name="merge",
    )(*map(pinned, kept), came, *pieces)


def combine_kernel(kept_a_ref, kept_b_ref, came_ref, *refs):
    parts, out_ref = refs[:-1], refs[-1]
    rows = out_ref.shape[0] // 2
    total = came_ref[0]
    for part in parts:
        total = total + part[...]
    count = total[4 * rows :]
    for ch in range(2):
        gain = total[ch * rows : (ch + 1) * rows]
        out_ref[ch * rows : (ch + 1) * rows, :] = (
            total[(2 + ch) * rows : (3 + ch) * rows] - count * gain
        )


def combine(kept, came, parts):
    rows = parts[0].shape[0] // 5
    return pl.pallas_call(
        combine_kernel,
        in_specs=[VMEM] * (3 + len(parts)),
        out_specs=VMEM,
        out_shape=jax.ShapeDtypeStruct((2 * rows, LANES), F32),
        compiler_params=pltpu.CompilerParams(vmem_limit_bytes=LIMIT),
        cost_estimate=pl.CostEstimate(flops=1 << 16, bytes_accessed=1 << 16, transcendentals=0),
        name="combine",
    )(*map(pinned, kept), came, *parts)


def product(n, kept_refs, js, parts):
    quarter = kept_refs[1].shape[0] // (n // 2)
    rows = quarter // LANES
    total = jnp.zeros((8, kept_refs[1].shape[1]), F32)
    for j, part in zip(js, parts):
        cols = [
            jnp.concatenate(
                [part[i : i + 1, :], part[rows + i : rows + i + 1, :], jnp.zeros((6, LANES), F32)],
                axis=0,
            )
            for i in range(rows)
        ]
        lhs = jnp.concatenate(cols, axis=1).astype(BF16)
        late, slot = 1 - j % 2, j // 2
        total = total + jnp.dot(
            lhs,
            kept_refs[late][slot * quarter : (slot + 1) * quarter, :],
            preferred_element_type=F32,
        )
    return total


def back_kernel(n, js, kept_a_ref, kept_b_ref, *refs):
    parts, before, out_ref = refs[: len(js)], refs[len(js) : -1], refs[-1]
    total = product(n, (kept_a_ref, kept_b_ref), js, parts)
    out_ref[...] = total + before[0][...] if before else total


def back(kept, js, parts, n, *before):
    quarter, markers = kept[1].shape[0] // (n // 2), kept[1].shape[1]
    return pl.pallas_call(
        functools.partial(back_kernel, n, js),
        in_specs=[VMEM] * (2 + len(js) + len(before)),
        out_specs=VMEM,
        out_shape=jax.ShapeDtypeStruct((8, markers), F32),
        compiler_params=pltpu.CompilerParams(vmem_limit_bytes=LIMIT),
        cost_estimate=pl.CostEstimate(
            flops=4 * quarter * markers * len(js),
            bytes_accessed=2 * quarter * markers * len(js),
            transcendentals=0,
        ),
        name="back",
    )(*map(pinned, kept), *parts, *before)


def back_last_kernel(n, js, kept_a_ref, kept_b_ref, before_ref, *refs):
    parts, (own_ref, other_ref, theirs_ref) = refs[:n], refs[n:]
    rows = parts[0].shape[0] // 2
    for j in range(n):
        theirs_ref[j * rows : (j + 1) * rows, :] = parts[j][rows : 2 * rows, :]
    total = before_ref[...] + product(n, (kept_a_ref, kept_b_ref), js, [parts[j] for j in js])
    for i in range(own_ref.shape[0]):
        own_ref[i : i + 1, :] = total[0:1, i * LANES : (i + 1) * LANES]
        other_ref[i : i + 1, :] = total[1:2, i * LANES : (i + 1) * LANES]


def back_last(kept, js, parts, n, before):
    quarter, markers = kept[1].shape[0] // (n // 2), kept[1].shape[1]
    grad = jax.ShapeDtypeStruct((markers // LANES, LANES), F32)
    return pl.pallas_call(
        functools.partial(back_last_kernel, n, js),
        in_specs=[VMEM] * (3 + n),
        out_specs=[VMEM] * 3,
        out_shape=[grad, grad, jax.ShapeDtypeStruct((n * quarter // LANES, LANES), F32)],
        compiler_params=pltpu.CompilerParams(vmem_limit_bytes=LIMIT),
        cost_estimate=pl.CostEstimate(
            flops=4 * quarter * markers * len(js),
            bytes_accessed=2 * quarter * markers * len(js),
            transcendentals=0,
        ),
        name="back_last",
    )(*map(pinned, kept), before, *parts)


def assemble_kernel(n, theirs_ref, *refs):
    parts, out_ref = refs[:n], refs[n]
    rows = parts[0].shape[0] // 2
    chain, rec = lax.axis_index("chain"), lax.axis_index("rec")
    for j in range(n):
        owner = rec ^ j
        out_ref[chain * n + owner] = parts[j][0:rows, :]
        out_ref[(1 - chain) * n + owner] = theirs_ref[j * rows : (j + 1) * rows, :]


def assemble(theirs, parts, n):
    rows = parts[0].shape[0] // 2
    return pl.pallas_call(
        functools.partial(assemble_kernel, n),
        in_specs=[VMEM] * (1 + n),
        out_specs=VMEM,
        out_shape=jax.ShapeDtypeStruct((2 * n, rows, LANES), F32),
        cost_estimate=pl.CostEstimate(flops=1 << 16, bytes_accessed=1 << 18, transcendentals=0),
        name="assemble",
    )(theirs, *parts)


def on_device(
    n_rec,
    n_ani,
    genotypes,
    effects,
    gaussian_draw,
    prior_prec,
    accept,
    herd_effect,
    phenotype,
    record_animal,
    record_bin,
    live_records,
):
    step_size = 0.005
    n = n_rec

    effects_2d, herd_2d = tiled(effects), tiled(herd_effect)
    theirs = (swap(effects_2d, "chain", 2, 1), swap(herd_2d, "chain", 2, 1))
    raw = prepare(
        herd_effect.shape[0],
        live_records.reshape(1, 1),
        tiled(record_animal),
        tiled(phenotype),
        tiled(record_bin),
    )
    theirs, raw = lax.optimization_barrier((theirs, raw))
    srcs = [raw] + [swap(raw, "ani", n_ani, j) for j in range(1, n_ani)]

    kept_a, gain_a = front_a(genotypes, [effects_2d, theirs[0]], n)
    kept_b, odd, rest = front_b(genotypes, kept_a, gain_a, [herd_2d, theirs[1]], srcs, n)
    kept = (kept_a, kept_b)
    came = swap(odd, "rec", n, 1)
    mine, *even = front_c(kept, rest, n)
    even = merge(kept, came, even)
    resid = combine(kept, came, [mine] + [swap(x, "rec", n, 2 * i + 2) for i, x in enumerate(even)])

    parts = [resid] + [swap(resid, "rec", n, j) for j in range(1, n)]
    grads = back(kept, [0], [resid], n)
    steps = [list(range(j, min(j + n // 4, n))) for j in range(1, n, n // 4)]
    for js in steps[:-1]:
        grads = back(kept, js, [parts[j] for j in js], n, grads)
    own, other, halves = back_last(kept, steps[-1], parts, n, grads)
    grad_part = own + swap(other, "chain", 2, 1)
    grad_part, swapped = lax.optimization_barrier((grad_part, swap(halves, "chain", 2, 1)))
    resid_sum = assemble(swapped, parts, n).reshape(-1)
    others = [shift(grad_part, "ani", n_ani, j) for j in range(1, n_ani)]

    likelihood_grad = grad_part
    for x in others:
        likelihood_grad = likelihood_grad + x
    likelihood_grad = likelihood_grad.reshape(-1)
    gradient = likelihood_grad - prior_prec * effects
    proposal = effects + step_size * gradient + math.sqrt(2.0 * step_size) * gaussian_draw
    accepted = jnp.repeat(accept, BLOCK) == 1
    return (jnp.where(accepted, proposal, effects), resid_sum)


def solution(mesh):
    return jax.shard_map(
        functools.partial(on_device, mesh.shape["rec"], mesh.shape["ani"]),
        mesh=mesh,
        in_specs=(
            P("ani", "rec"),
            P(("chain", "rec")),
            P(("chain", "rec")),
            P("rec"),
            P(("chain", "rec")),
            P(("chain", "rec")),
            P(("rec", "ani")),
            P(("rec", "ani")),
            P(("rec", "ani")),
            P(("rec", "ani")),
        ),
        out_specs=(P(("chain", "rec")), P(("chain", "ani"))),
        check_vma=False,
    )
```

```python
import functools
import math

import jax
import jax.numpy as jnp
from jax import lax
from jax.experimental import pallas as pl
from jax.experimental.pallas import tpu as pltpu
from jax.sharding import PartitionSpec as P

BLOCK = 128
LANES = 128
SUBS = 64
SPAN_BITS = 14
CHUNK_ROWS = 16
LIMIT = 14 << 20
F32 = jnp.float32
BF16 = jnp.bfloat16
NT = (((1,), (1,)), ((), ()))
VMEM = pl.BlockSpec(memory_space=pltpu.VMEM)
SMEM = pl.BlockSpec(memory_space=pltpu.SMEM)
ANY = pl.BlockSpec(memory_space=pl.ANY)


def swap(x, axis, size, j):
    return lax.ppermute(x, axis, [(i, i ^ j) for i in range(size)])


def shift(x, axis, size, j):
    return lax.ppermute(x, axis, [(i, (i + j) % size) for i in range(size)])


def tiled(x):
    return x.reshape(-1, LANES)


def locate(j, n):
    i = j // 2
    if j % 2:
        return (0, i) if i < n // 4 else (1, i - n // 4)
    return (1, n // 4 + i) if i < n // 4 else (2, i - n // 4)


def load(j, n, g_hbm, kept_ref, sem):
    chain, rec = lax.axis_index("chain"), lax.axis_index("rec")
    half = g_hbm.shape[0] // 2
    quarter = half // n
    slot = locate(j, n)[1]
    at = pl.multiple_of(chain * half + (rec ^ j) * quarter, quarter)
    return pltpu.make_async_copy(
        g_hbm.at[pl.ds(at, quarter), :],
        kept_ref.at[slot * quarter : (slot + 1) * quarter, :],
        sem.at[slot],
    )


def prepare_kernel(bins, n, live_ref, animal_any, y_any, bin_any, g_hbm, kept_ref, raw_any, *scratch):
    *small_s, raw_s, sem, small_sem, raw_sem = scratch
    small = [
        pltpu.make_async_copy(a, b, small_sem.at[k])
        for k, (a, b) in enumerate(zip((animal_any, y_any, bin_any), small_s))
    ]
    for copy in small:
        copy.start()
    big = [load(2 * i + 1, n, g_hbm, kept_ref, sem) for i in range(n // 4)]
    for copy in big:
        copy.start()
    for copy in small:
        copy.wait()
    animal, y, which = small_s
    rows = animal.shape[0]
    slot = (
        lax.broadcasted_iota(jnp.int32, (rows, LANES), 0) * LANES
        + lax.broadcasted_iota(jnp.int32, (rows, LANES), 1)
    )
    raw_s[0:rows, :] = jnp.where(slot < live_ref[0], animal[...], -1).astype(F32)
    raw_s[rows : 2 * rows, :] = y[...]
    raw_s[2 * rows : 3 * rows, :] = (which[...] - lax.axis_index("rec") * bins).astype(F32)
    out = pltpu.make_async_copy(raw_s, raw_any, raw_sem)
    out.start()
    for copy in big:
        copy.wait()
    out.wait()


def in_hbm(arrays):
    return [pltpu.with_memory_space_constraint(x, pltpu.HBM) for x in arrays]


def prepare(genotypes, bins, n, live, animal, y, which):
    rows = animal.shape[0]
    block, markers = genotypes.shape
    return pl.pallas_call(
        functools.partial(prepare_kernel, bins, n),
        in_specs=[SMEM] + [ANY] * 4,
        out_specs=[VMEM, ANY],
        out_shape=[pltpu.VMEM((block // 8, markers), BF16), pltpu.HBM((3 * rows, LANES), F32)],
        scratch_shapes=[
            pltpu.VMEM((rows, LANES), jnp.int32),
            pltpu.VMEM((rows, LANES), F32),
            pltpu.VMEM((rows, LANES), jnp.int32),
            pltpu.VMEM((3 * rows, LANES), F32),
            pltpu.SemaphoreType.DMA((n // 4,)),
            pltpu.SemaphoreType.DMA((3,)),
            pltpu.SemaphoreType.DMA,
        ],
        compiler_params=pltpu.CompilerParams(vmem_limit_bytes=LIMIT),
        cost_estimate=pl.CostEstimate(
            flops=1 << 16, bytes_accessed=block * markers // 4, transcendentals=0
        ),
        name="prepare",
    )(live, *in_hbm([animal, y, which]), genotypes)


def up(x, k):
    return jnp.concatenate([x[k:], jnp.zeros((k,) + x.shape[1:], x.dtype)], axis=0)


def down(x, k):
    return jnp.concatenate([jnp.zeros((k,) + x.shape[1:], x.dtype), x[:-k]], axis=0)


def compact(srcs, base, key_s, y_s):
    src_rows = srcs[0].shape[0] // 3
    keys, ys = [], []
    for src in srcs:
        local = src[0:src_rows, :].astype(jnp.int32) - base
        which = src[2 * src_rows : 3 * src_rows, :].astype(jnp.int32)
        known = (local >= 0) & (local < (1 << SPAN_BITS))
        keys.append(jnp.where(known, (which << SPAN_BITS) + local, -1))
        ys.append(src[src_rows : 2 * src_rows, :])
    key = jnp.concatenate(keys, axis=0)
    y = jnp.concatenate(ys, axis=0)
    total = key.shape[0]
    gone = jnp.where(key < 0, 1, 0)
    left = gone
    k = 1
    while k < total:
        left = left + down(left, k)
        k *= 2
    most = total - jnp.min(left[total - 1 : total, :])
    left = left - gone
    k = 1
    while k < total:
        move = (key >= 0) & ((left & k) != 0)
        key_up = up(jnp.where(move, key, -1), k)
        key_up = jnp.concatenate([key_up[: total - k], jnp.full((k, LANES), -1, jnp.int32)], axis=0)
        come = key_up >= 0
        key = jnp.where(come, key_up, jnp.where(move, -1, key))
        y = jnp.where(come, up(y, k), y)
        left = jnp.where(come, up(left, k), left)
        k *= 2
    key_s[...] = key
    y_s[...] = y
    return most


def look_up(t, herds, key_s, y_s, lane_s, sub_s, v_s):
    for g in range(CHUNK_ROWS // 8):
        at = pl.ds(pl.multiple_of(t * CHUNK_ROWS + g * 8, 8), 8)
        key, y = key_s[at, :], y_s[at, :]
        local, which = key & ((1 << SPAN_BITS) - 1), key >> SPAN_BITS
        lane = (local & (LANES - 1)) | ((local >> 13) << 7)
        lane_s[at, :] = jnp.where(key >= 0, lane, -1).astype(F32)
        sub_s[at, :] = ((local >> 7) & (SUBS - 1)).astype(F32)
        low, high = which & (LANES - 1), which >> 7
        for ch, ref in enumerate(herds):
            found = jnp.zeros((8, LANES), F32)
            for q in range(ref.shape[0]):
                row = jnp.broadcast_to(ref[q : q + 1, :], (8, LANES))
                got = jnp.take_along_axis(row, low, axis=1, mode="promise_in_bounds")
                found = jnp.where(high == q, got, found)
            value = y - found
            upper = value.astype(BF16).astype(F32)
            v_s[2 * ch, at, :] = upper
            v_s[2 * ch + 1, at, :] = value - upper


def spread(row, count):
    few = jnp.broadcast_to(row, (16, LANES)).astype(BF16)
    return jnp.broadcast_to(few[None], (count // 16, 16, LANES)).reshape(count, LANES)


def one_hots(t, lane_s, sub_s, v_s, lanes_iota, subs_iota):
    a_cols, b_cols = [], []
    one, zero = jnp.ones((), BF16), jnp.zeros((), BF16)
    for i in range(CHUNK_ROWS):
        at = pl.ds(t * CHUNK_ROWS + i, 1)
        a_cols.append(jnp.where(lanes_iota == spread(lane_s[at, :], 2 * LANES), one, zero))
        mask = subs_iota == spread(sub_s[at, :], SUBS)
        pieces = [jnp.where(mask, spread(v_s[p, at, :], SUBS), zero) for p in range(4)]
        pieces.append(jnp.where(mask, one, zero))
        b_cols.append(jnp.concatenate(pieces, axis=0))
    return jnp.concatenate(b_cols, axis=1), jnp.concatenate(a_cols, axis=1)


def gains(e2, kept_ref, at, count, out_ref, row, rows):
    res = lax.dot_general(e2, kept_ref[pl.ds(at, count), :], NT, preferred_element_type=F32)
    for i in range(count // LANES):
        for ch in range(2):
            out_ref[pl.ds(ch * rows + row + i, 1), :] = res[
                ch : ch + 1, i * LANES : (i + 1) * LANES
            ]


def front_a_kernel(n, kept_0_ref, own_any, other_any, g_hbm, kept_ref, gains_any, gain, own_s, other_s, sem, small_sem, out_sem):
    markers = kept_ref.shape[1]
    quarter = (kept_ref.shape[0] - 16) // (n // 2)
    rows = quarter // LANES
    small = [
        pltpu.make_async_copy(a, b, small_sem.at[k])
        for k, (a, b) in enumerate([(own_any, own_s), (other_any, other_s)])
    ]
    for copy in small:
        copy.start()
    odd = [load(2 * i + 1, n, g_hbm, kept_ref, sem) for i in range(n // 4, n // 2)]
    even = [load(2 * i, n, g_hbm, kept_ref, sem) for i in range(n // 4)]
    for copy in odd + even:
        copy.start()
    for copy in small:
        copy.wait()
    e2 = jnp.concatenate(
        [
            jnp.concatenate([ref[i : i + 1, :] for i in range(markers // LANES)], axis=1)
            for ref in (own_s, other_s)
        ]
        + [jnp.zeros((14, markers), F32)],
        axis=0,
    ).astype(BF16)
    kept_ref[(n // 2) * quarter :, :] = e2
    for i in range(n // 4):
        gains(e2[:8], kept_0_ref, i * quarter, quarter, gain.at[i], 0, rows)
    for i in range(n // 4):
        odd[i].wait()
        gains(e2[:8], kept_ref, i * quarter, quarter, gain.at[n // 4 + i], 0, rows)
    done = pltpu.make_async_copy(gain, gains_any, out_sem)
    done.start()
    for copy in even:
        copy.wait()
    done.wait()


def front_a(genotypes, kept_0, effects, n):
    block, markers = genotypes.shape
    half = block // 2
    quarter = half // n
    rows = quarter // LANES
    shape = (n // 2, 2 * rows, LANES)
    return pl.pallas_call(
        functools.partial(front_a_kernel, n),
        in_specs=[VMEM] + [ANY] * 3,
        out_specs=[VMEM, ANY],
        out_shape=[pltpu.VMEM((n // 2 * quarter + 16, markers), BF16), pltpu.HBM(shape, F32)],
        scratch_shapes=[
            pltpu.VMEM(shape, F32),
            pltpu.VMEM(effects[0].shape, F32),
            pltpu.VMEM(effects[1].shape, F32),
            pltpu.SemaphoreType.DMA((n // 2,)),
            pltpu.SemaphoreType.DMA((2,)),
            pltpu.SemaphoreType.DMA,
        ],
        compiler_params=pltpu.CompilerParams(vmem_limit_bytes=LIMIT),
        cost_estimate=pl.CostEstimate(
            flops=2 * half * markers, bytes_accessed=half * markers, transcendentals=0
        ),
        name="front_a",
    )(pinned(kept_0), *in_hbm(effects), genotypes)


def front_b_kernel(n, n_src, kept_0_ref, kept_a_ref, *refs):
    small_any, g_hbm = refs[: n_src + 3], refs[n_src + 3]
    kept_ref, odd, rest = refs[n_src + 4 : n_src + 7]
    key_s, y_s, lane_s, sub_s, v_s, acc, tab, *small_s, sem, small_sem = refs[n_src + 7 :]
    quarter = kept_ref.shape[0] // (n // 4)
    half = quarter * n
    rows = quarter // LANES
    chain, rec, ani = lax.axis_index("chain"), lax.axis_index("rec"), lax.axis_index("ani")

    small = [
        pltpu.make_async_copy(a, b, small_sem.at[k])
        for k, (a, b) in enumerate(zip(small_any, small_s))
    ]
    for copy in small:
        copy.start()
    big = [load(2 * i, n, g_hbm, kept_ref, sem) for i in range(n // 4, n // 2)]
    for copy in big:
        copy.start()
    for copy in small:
        copy.wait()
    srcs, (*herds, gain_a) = small_s[:n_src], small_s[n_src:]

    most = compact(srcs, ani * 2 * half + chain * half, key_s, y_s)
    acc[...] = jnp.zeros_like(acc)
    lanes_iota = lax.broadcasted_iota(jnp.int32, (2 * LANES, LANES), 0).astype(F32).astype(BF16)
    subs_iota = lax.broadcasted_iota(jnp.int32, (SUBS, LANES), 0).astype(F32).astype(BF16)

    @pl.loop(0, (most + CHUNK_ROWS - 1) // CHUNK_ROWS)
    def _(t):
        look_up(t, herds, key_s, y_s, lane_s, sub_s, v_s)
        b, a = one_hots(t, lane_s, sub_s, v_s, lanes_iota, subs_iota)
        acc[...] += lax.dot_general(b, a, NT, preferred_element_type=F32)

    for q in range(n):
        wide, first = divmod(q * rows, SUBS)
        cols = slice(wide * LANES, (wide + 1) * LANES)
        window = lambda p: acc[p * SUBS + first : p * SUBS + first + rows, cols]
        tab[q, 0:rows, :] = window(0) + window(1)
        tab[q, rows : 2 * rows, :] = window(2) + window(3)
        tab[q, 2 * rows : 3 * rows, :] = window(4)
    for i in range(n // 2):
        rest[i] = tab[rec ^ (2 * i)]
        odd[i, 2 * rows : 5 * rows, :] = tab[rec ^ (2 * i + 1)]
        odd[i, 0 : 2 * rows, :] = gain_a[i]
    for copy in big:
        copy.wait()


def front_b(genotypes, kept, gain_a, herds, srcs, n):
    block, markers = genotypes.shape
    half = block // 2
    quarter = half // n
    total = len(srcs) * srcs[0].shape[0] // 3
    rows = quarter // LANES
    small = [*srcs, *herds, gain_a]
    return pl.pallas_call(
        functools.partial(front_b_kernel, n, len(srcs)),
        in_specs=[VMEM] * 2 + [ANY] * (1 + len(small)),
        out_specs=[VMEM] * 3,
        out_shape=[
            pltpu.VMEM((n // 4 * quarter, markers), BF16),
            jax.ShapeDtypeStruct((n // 2, 5 * rows, LANES), F32),
            jax.ShapeDtypeStruct((n // 2, 3 * rows, LANES), F32),
        ],
        scratch_shapes=[
            pltpu.VMEM((total, LANES), jnp.int32),
            pltpu.VMEM((total, LANES), F32),
            pltpu.VMEM((total, LANES), F32),
            pltpu.VMEM((total, LANES), F32),
            pltpu.VMEM((4, total, LANES), F32),
            pltpu.VMEM((5 * SUBS, 2 * LANES), F32),
            pltpu.VMEM((n, 3 * rows, LANES), F32),
        ]
        + [pltpu.VMEM(x.shape, F32) for x in small]
        + [pltpu.SemaphoreType.DMA((n // 4,)), pltpu.SemaphoreType.DMA((len(small),))],
        compiler_params=pltpu.CompilerParams(vmem_limit_bytes=LIMIT),
        cost_estimate=pl.CostEstimate(
            flops=4 * half * markers, bytes_accessed=half * markers, transcendentals=0
        ),
        name="front_b",
    )(
        *map(pinned, kept),
        *in_hbm(small),
        genotypes,
    )


def pinned(x):
    return pltpu.with_memory_space_constraint(x, pltpu.VMEM)


def front_c_kernel(n, kept_0_ref, kept_a_ref, kept_b_ref, rest_ref, *outs):
    quarter = kept_b_ref.shape[0] // (n // 4)
    rows = quarter // LANES
    e2 = kept_a_ref[n // 2 * quarter : n // 2 * quarter + 8, :]
    for i in range(n // 2):
        outs[i][2 * rows : 5 * rows, :] = rest_ref[i]
        late, slot = locate(2 * i, n)
        kept_ref = (kept_0_ref, kept_a_ref, kept_b_ref)[late]
        gains(e2, kept_ref, slot * quarter, quarter, outs[i], 0, rows)


def front_c(kept, rest, n):
    quarter, markers = kept[2].shape[0] // (n // 4), kept[2].shape[1]
    piece = jax.ShapeDtypeStruct((5 * quarter // LANES, LANES), F32)
    return pl.pallas_call(
        functools.partial(front_c_kernel, n),
        in_specs=[VMEM] * 4,
        out_specs=[VMEM] * (n // 2),
        out_shape=[piece] * (n // 2),
        compiler_params=pltpu.CompilerParams(vmem_limit_bytes=LIMIT),
        cost_estimate=pl.CostEstimate(
            flops=2 * n * quarter * markers, bytes_accessed=n * quarter * markers, transcendentals=0
        ),
        name="front_c",
    )(*map(pinned, kept), rest)


def merge_kernel(kept_0_ref, kept_a_ref, kept_b_ref, came_ref, *refs):
    count = len(refs) // 2
    for i in range(count):
        refs[count + i][...] = refs[i][...] + came_ref[i + 1]


def merge(kept, came, pieces):
    return pl.pallas_call(
        merge_kernel,
        in_specs=[VMEM] * (4 + len(pieces)),
        out_specs=[VMEM] * len(pieces),
        out_shape=[jax.ShapeDtypeStruct(x.shape, F32) for x in pieces],
        compiler_params=pltpu.CompilerParams(vmem_limit_bytes=LIMIT),
        cost_estimate=pl.CostEstimate(flops=1 << 16, bytes_accessed=1 << 16, transcendentals=0),
        name="merge",
    )(*map(pinned, kept), came, *pieces)


def combine_kernel(kept_0_ref, kept_a_ref, kept_b_ref, came_ref, *refs):
    parts, out_ref = refs[:-1], refs[-1]
    rows = out_ref.shape[0] // 2
    total = came_ref[0]
    for part in parts:
        total = total + part[...]
    count = total[4 * rows :]
    for ch in range(2):
        gain = total[ch * rows : (ch + 1) * rows]
        out_ref[ch * rows : (ch + 1) * rows, :] = (
            total[(2 + ch) * rows : (3 + ch) * rows] - count * gain
        )


def combine(kept, came, parts):
    rows = parts[0].shape[0] // 5
    return pl.pallas_call(
        combine_kernel,
        in_specs=[VMEM] * (4 + len(parts)),
        out_specs=VMEM,
        out_shape=jax.ShapeDtypeStruct((2 * rows, LANES), F32),
        compiler_params=pltpu.CompilerParams(vmem_limit_bytes=LIMIT),
        cost_estimate=pl.CostEstimate(flops=1 << 16, bytes_accessed=1 << 16, transcendentals=0),
        name="combine",
    )(*map(pinned, kept), came, *parts)


def product(n, kept_refs, js, parts):
    quarter = kept_refs[2].shape[0] // (n // 4)
    rows = quarter // LANES
    total = jnp.zeros((8, kept_refs[1].shape[1]), F32)
    for j, part in zip(js, parts):
        cols = [
            jnp.concatenate(
                [part[i : i + 1, :], part[rows + i : rows + i + 1, :], jnp.zeros((6, LANES), F32)],
                axis=0,
            )
            for i in range(rows)
        ]
        lhs = jnp.concatenate(cols, axis=1).astype(BF16)
        late, slot = locate(j, n)
        total = total + jnp.dot(
            lhs,
            kept_refs[late][slot * quarter : (slot + 1) * quarter, :],
            preferred_element_type=F32,
        )
    return total


def back_kernel(n, js, kept_0_ref, kept_a_ref, kept_b_ref, *refs):
    parts, before, out_ref = refs[: len(js)], refs[len(js) : -1], refs[-1]
    total = product(n, (kept_0_ref, kept_a_ref, kept_b_ref), js, parts)
    out_ref[...] = total + before[0][...] if before else total


def back(kept, js, parts, n, *before):
    quarter, markers = kept[2].shape[0] // (n // 4), kept[2].shape[1]
    return pl.pallas_call(
        functools.partial(back_kernel, n, js),
        in_specs=[VMEM] * (3 + len(js) + len(before)),
        out_specs=VMEM,
        out_shape=jax.ShapeDtypeStruct((8, markers), F32),
        compiler_params=pltpu.CompilerParams(vmem_limit_bytes=LIMIT),
        cost_estimate=pl.CostEstimate(
            flops=4 * quarter * markers * len(js),
            bytes_accessed=2 * quarter * markers * len(js),
            transcendentals=0,
        ),
        name="back",
    )(*map(pinned, kept), *parts, *before)


def back_last_kernel(n, js, kept_0_ref, kept_a_ref, kept_b_ref, before_ref, *refs):
    parts, (own_ref, other_ref, theirs_ref) = refs[:n], refs[n:]
    rows = parts[0].shape[0] // 2
    for j in range(n):
        theirs_ref[j * rows : (j + 1) * rows, :] = parts[j][rows : 2 * rows, :]
    total = before_ref[...] + product(n, (kept_0_ref, kept_a_ref, kept_b_ref), js, [parts[j] for j in js])
    for i in range(own_ref.shape[0]):
        own_ref[i : i + 1, :] = total[0:1, i * LANES : (i + 1) * LANES]
        other_ref[i : i + 1, :] = total[1:2, i * LANES : (i + 1) * LANES]


def back_last(kept, js, parts, n, before):
    quarter, markers = kept[2].shape[0] // (n // 4), kept[2].shape[1]
    grad = jax.ShapeDtypeStruct((markers // LANES, LANES), F32)
    return pl.pallas_call(
        functools.partial(back_last_kernel, n, js),
        in_specs=[VMEM] * (4 + n),
        out_specs=[VMEM] * 3,
        out_shape=[grad, grad, jax.ShapeDtypeStruct((n * quarter // LANES, LANES), F32)],
        compiler_params=pltpu.CompilerParams(vmem_limit_bytes=LIMIT),
        cost_estimate=pl.CostEstimate(
            flops=4 * quarter * markers * len(js),
            bytes_accessed=2 * quarter * markers * len(js),
            transcendentals=0,
        ),
        name="back_last",
    )(*map(pinned, kept), before, *parts)


def assemble_kernel(n, theirs_ref, *refs):
    parts, out_ref = refs[:n], refs[n]
    rows = parts[0].shape[0] // 2
    chain, rec = lax.axis_index("chain"), lax.axis_index("rec")
    for j in range(n):
        owner = rec ^ j
        out_ref[chain * n + owner] = parts[j][0:rows, :]
        out_ref[(1 - chain) * n + owner] = theirs_ref[j * rows : (j + 1) * rows, :]


def assemble(theirs, parts, n):
    rows = parts[0].shape[0] // 2
    return pl.pallas_call(
        functools.partial(assemble_kernel, n),
        in_specs=[VMEM] * (1 + n),
        out_specs=VMEM,
        out_shape=jax.ShapeDtypeStruct((2 * n, rows, LANES), F32),
        cost_estimate=pl.CostEstimate(flops=1 << 16, bytes_accessed=1 << 18, transcendentals=0),
        name="assemble",
    )(theirs, *parts)


def on_device(
    n_rec,
    n_ani,
    genotypes,
    effects,
    gaussian_draw,
    prior_prec,
    accept,
    herd_effect,
    phenotype,
    record_animal,
    record_bin,
    live_records,
):
    step_size = 0.005
    n = n_rec

    effects_2d, herd_2d = tiled(effects), tiled(herd_effect)
    theirs = (swap(effects_2d, "chain", 2, 1), swap(herd_2d, "chain", 2, 1))
    kept_0, raw = prepare(
        genotypes,
        herd_effect.shape[0],
        n,
        live_records,
        tiled(record_animal),
        tiled(phenotype),
        tiled(record_bin),
    )
    theirs, raw = lax.optimization_barrier((theirs, raw))
    srcs = [raw] + [swap(raw, "ani", n_ani, j) for j in range(1, n_ani)]

    kept_a, gain_a = front_a(genotypes, kept_0, [effects_2d, theirs[0]], n)
    kept_b, odd, rest = front_b(genotypes, (kept_0, kept_a), gain_a, [herd_2d, theirs[1]], srcs, n)
    kept = (kept_0, kept_a, kept_b)
    came = swap(odd, "rec", n, 1)
    mine, *even = front_c(kept, rest, n)
    even = merge(kept, came, even)
    resid = combine(kept, came, [mine] + [swap(x, "rec", n, 2 * i + 2) for i, x in enumerate(even)])

    parts = [resid] + [swap(resid, "rec", n, j) for j in range(1, n)]
    grads = back(kept, [0], [resid], n)
    steps = [list(range(j, min(j + n // 4, n))) for j in range(1, n, n // 4)]
    for js in steps[:-1]:
        grads = back(kept, js, [parts[j] for j in js], n, grads)
    own, other, halves = back_last(kept, steps[-1], parts, n, grads)
    grad_part = own + swap(other, "chain", 2, 1)
    grad_part, swapped = lax.optimization_barrier((grad_part, swap(halves, "chain", 2, 1)))
    resid_sum = assemble(swapped, parts, n).reshape(-1)
    others = [shift(grad_part, "ani", n_ani, j) for j in range(1, n_ani)]

    likelihood_grad = grad_part
    for x in others:
        likelihood_grad = likelihood_grad + x
    likelihood_grad = likelihood_grad.reshape(-1)
    gradient = likelihood_grad - prior_prec * effects
    proposal = effects + step_size * gradient + math.sqrt(2.0 * step_size) * gaussian_draw
    accepted = jnp.repeat(accept, BLOCK) == 1
    return (jnp.where(accepted, proposal, effects), resid_sum)


def solution(mesh):
    return jax.shard_map(
        functools.partial(on_device, mesh.shape["rec"], mesh.shape["ani"]),
        mesh=mesh,
        in_specs=(
            P("ani", "rec"),
            P(("chain", "rec")),
            P(("chain", "rec")),
            P("rec"),
            P(("chain", "rec")),
            P(("chain", "rec")),
            P(("rec", "ani")),
            P(("rec", "ani")),
            P(("rec", "ani")),
            P(("rec", "ani")),
        ),
        out_specs=(P(("chain", "rec")), P(("chain", "ani"))),
        check_vma=False,
    )
```

```python
import functools
import math

import jax
import jax.numpy as jnp
from jax import lax
from jax.experimental import pallas as pl
from jax.experimental.pallas import tpu as pltpu
from jax.sharding import PartitionSpec as P

BLOCK = 128
LANES = 128
SUBS = 64
SPAN_BITS = 14
CHUNK_ROWS = 16
LIMIT = 14 << 20
F32 = jnp.float32
BF16 = jnp.bfloat16
NT = (((1,), (1,)), ((), ()))
VMEM = pl.BlockSpec(memory_space=pltpu.VMEM)
SMEM = pl.BlockSpec(memory_space=pltpu.SMEM)
ANY = pl.BlockSpec(memory_space=pl.ANY)


def swap(x, axis, size, j):
    return lax.ppermute(x, axis, [(i, i ^ j) for i in range(size)])


def shift(x, axis, size, j):
    return lax.ppermute(x, axis, [(i, (i + j) % size) for i in range(size)])


def tiled(x):
    return x.reshape(-1, LANES)


def locate(j, n):
    i = j // 2
    if j % 2:
        return (0, i) if i < n // 4 else (1, i - n // 4)
    return (1, n // 4 + i) if i < n // 4 else (2, i - n // 4)


def load(j, n, g_hbm, kept_ref, sem):
    chain, rec = lax.axis_index("chain"), lax.axis_index("rec")
    half = g_hbm.shape[0] // 2
    quarter = half // n
    slot = locate(j, n)[1]
    at = pl.multiple_of(chain * half + (rec ^ j) * quarter, quarter)
    return pltpu.make_async_copy(
        g_hbm.at[pl.ds(at, quarter), :],
        kept_ref.at[slot * quarter : (slot + 1) * quarter, :],
        sem.at[slot],
    )


def prepare_kernel(bins, n, live_ref, animal_any, y_any, bin_any, g_hbm, kept_ref, raw_any, *scratch):
    *small_s, raw_s, sem, small_sem, raw_sem = scratch
    small = [
        pltpu.make_async_copy(a, b, small_sem.at[k])
        for k, (a, b) in enumerate(zip((animal_any, y_any, bin_any), small_s))
    ]
    for copy in small:
        copy.start()
    big = [load(2 * i + 1, n, g_hbm, kept_ref, sem) for i in range(n // 4)]
    for copy in big:
        copy.start()
    for copy in small:
        copy.wait()
    animal, y, which = small_s
    rows = animal.shape[0]
    slot = (
        lax.broadcasted_iota(jnp.int32, (rows, LANES), 0) * LANES
        + lax.broadcasted_iota(jnp.int32, (rows, LANES), 1)
    )
    raw_s[0:rows, :] = jnp.where(slot < live_ref[0], animal[...], -1).astype(F32)
    raw_s[rows : 2 * rows, :] = y[...]
    raw_s[2 * rows : 3 * rows, :] = (which[...] - lax.axis_index("rec") * bins).astype(F32)
    out = pltpu.make_async_copy(raw_s, raw_any, raw_sem)
    out.start()
    for copy in big:
        copy.wait()
    out.wait()


def in_hbm(arrays):
    return [pltpu.with_memory_space_constraint(x, pltpu.HBM) for x in arrays]


def prepare(genotypes, bins, n, live, animal, y, which):
    rows = animal.shape[0]
    block, markers = genotypes.shape
    return pl.pallas_call(
        functools.partial(prepare_kernel, bins, n),
        in_specs=[SMEM] + [ANY] * 4,
        out_specs=[VMEM, ANY],
        out_shape=[pltpu.VMEM((block // 8, markers), BF16), pltpu.HBM((3 * rows, LANES), F32)],
        scratch_shapes=[
            pltpu.VMEM((rows, LANES), jnp.int32),
            pltpu.VMEM((rows, LANES), F32),
            pltpu.VMEM((rows, LANES), jnp.int32),
            pltpu.VMEM((3 * rows, LANES), F32),
            pltpu.SemaphoreType.DMA((n // 4,)),
            pltpu.SemaphoreType.DMA((3,)),
            pltpu.SemaphoreType.DMA,
        ],
        compiler_params=pltpu.CompilerParams(vmem_limit_bytes=LIMIT),
        cost_estimate=pl.CostEstimate(
            flops=1 << 16, bytes_accessed=block * markers // 4, transcendentals=0
        ),
        name="prepare",
    )(live, *in_hbm([animal, y, which]), genotypes)


def up(x, k):
    return jnp.concatenate([x[k:], jnp.zeros((k,) + x.shape[1:], x.dtype)], axis=0)


def down(x, k):
    return jnp.concatenate([jnp.zeros((k,) + x.shape[1:], x.dtype), x[:-k]], axis=0)


def compact(srcs, base, key_s, y_s):
    src_rows = srcs[0].shape[0] // 3
    keys, ys = [], []
    for src in srcs:
        local = src[0:src_rows, :].astype(jnp.int32) - base
        which = src[2 * src_rows : 3 * src_rows, :].astype(jnp.int32)
        known = (local >= 0) & (local < (1 << SPAN_BITS))
        keys.append(jnp.where(known, (which << SPAN_BITS) + local, -1))
        ys.append(src[src_rows : 2 * src_rows, :])
    key = jnp.concatenate(keys, axis=0)
    y = jnp.concatenate(ys, axis=0)
    total = key.shape[0]
    gone = jnp.where(key < 0, 1, 0)
    left = gone
    k = 1
    while k < total:
        left = left + down(left, k)
        k *= 2
    most = total - jnp.min(left[total - 1 : total, :])
    left = left - gone
    k = 1
    while k < total:
        move = (key >= 0) & ((left & k) != 0)
        key_up = up(jnp.where(move, key, -1), k)
        key_up = jnp.concatenate([key_up[: total - k], jnp.full((k, LANES), -1, jnp.int32)], axis=0)
        come = key_up >= 0
        key = jnp.where(come, key_up, jnp.where(move, -1, key))
        y = jnp.where(come, up(y, k), y)
        left = jnp.where(come, up(left, k), left)
        k *= 2
    key_s[...] = key
    y_s[...] = y
    return most


def look_up(t, herds, key_s, y_s, lane_s, sub_s, v_s):
    for g in range(CHUNK_ROWS // 8):
        at = pl.ds(pl.multiple_of(t * CHUNK_ROWS + g * 8, 8), 8)
        key, y = key_s[at, :], y_s[at, :]
        local, which = key & ((1 << SPAN_BITS) - 1), key >> SPAN_BITS
        lane = (local & (LANES - 1)) | ((local >> 13) << 7)
        lane_s[at, :] = jnp.where(key >= 0, lane, -1).astype(F32)
        sub_s[at, :] = ((local >> 7) & (SUBS - 1)).astype(F32)
        low, high = which & (LANES - 1), which >> 7
        for ch, ref in enumerate(herds):
            found = jnp.zeros((8, LANES), F32)
            for q in range(ref.shape[0]):
                row = jnp.broadcast_to(ref[q : q + 1, :], (8, LANES))
                got = jnp.take_along_axis(row, low, axis=1, mode="promise_in_bounds")
                found = jnp.where(high == q, got, found)
            value = y - found
            upper = value.astype(BF16).astype(F32)
            v_s[2 * ch, at, :] = upper
            v_s[2 * ch + 1, at, :] = value - upper


def spread(row, count):
    few = jnp.broadcast_to(row, (16, LANES)).astype(BF16)
    return jnp.broadcast_to(few[None], (count // 16, 16, LANES)).reshape(count, LANES)


def one_hots(t, lane_s, sub_s, v_s, lanes_iota, subs_iota):
    a_cols, b_cols = [], []
    one, zero = jnp.ones((), BF16), jnp.zeros((), BF16)
    for i in range(CHUNK_ROWS):
        at = pl.ds(t * CHUNK_ROWS + i, 1)
        a_cols.append(jnp.where(lanes_iota == spread(lane_s[at, :], 2 * LANES), one, zero))
        mask = subs_iota == spread(sub_s[at, :], SUBS)
        pieces = [jnp.where(mask, spread(v_s[p, at, :], SUBS), zero) for p in range(4)]
        pieces.append(jnp.where(mask, one, zero))
        b_cols.append(jnp.concatenate(pieces, axis=0))
    return jnp.concatenate(b_cols, axis=1), jnp.concatenate(a_cols, axis=1)


def gains(e2, kept_ref, at, count, out_ref, row, rows):
    res = lax.dot_general(e2, kept_ref[pl.ds(at, count), :], NT, preferred_element_type=F32)
    for i in range(count // LANES):
        for ch in range(2):
            out_ref[pl.ds(ch * rows + row + i, 1), :] = res[
                ch : ch + 1, i * LANES : (i + 1) * LANES
            ]


def front_a_kernel(n, kept_0_ref, own_any, other_any, g_hbm, kept_ref, gains_any, gain, own_s, other_s, sem, small_sem, out_sem):
    markers = kept_ref.shape[1]
    quarter = (kept_ref.shape[0] - 16) // (n // 2)
    rows = quarter // LANES
    small = [
        pltpu.make_async_copy(a, b, small_sem.at[k])
        for k, (a, b) in enumerate([(own_any, own_s), (other_any, other_s)])
    ]
    for copy in small:
        copy.start()
    odd = [load(2 * i + 1, n, g_hbm, kept_ref, sem) for i in range(n // 4, n // 2)]
    even = [load(2 * i, n, g_hbm, kept_ref, sem) for i in range(n // 4)]
    for copy in odd + even:
        copy.start()
    for copy in small:
        copy.wait()
    e2 = jnp.concatenate(
        [
            jnp.concatenate([ref[i : i + 1, :] for i in range(markers // LANES)], axis=1)
            for ref in (own_s, other_s)
        ]
        + [jnp.zeros((14, markers), F32)],
        axis=0,
    ).astype(BF16)
    kept_ref[(n // 2) * quarter :, :] = e2
    for i in range(n // 4):
        gains(e2[:8], kept_0_ref, i * quarter, quarter, gain.at[i], 0, rows)
    for i in range(n // 4):
        odd[i].wait()
        gains(e2[:8], kept_ref, i * quarter, quarter, gain.at[n // 4 + i], 0, rows)
    done = pltpu.make_async_copy(gain, gains_any, out_sem)
    done.start()
    for copy in even:
        copy.wait()
    done.wait()


def front_a(genotypes, kept_0, effects, n):
    block, markers = genotypes.shape
    half = block // 2
    quarter = half // n
    rows = quarter // LANES
    shape = (n // 2, 2 * rows, LANES)
    return pl.pallas_call(
        functools.partial(front_a_kernel, n),
        in_specs=[VMEM] + [ANY] * 3,
        out_specs=[VMEM, ANY],
        out_shape=[pltpu.VMEM((n // 2 * quarter + 16, markers), BF16), pltpu.HBM(shape, F32)],
        scratch_shapes=[
            pltpu.VMEM(shape, F32),
            pltpu.VMEM(effects[0].shape, F32),
            pltpu.VMEM(effects[1].shape, F32),
            pltpu.SemaphoreType.DMA((n // 2,)),
            pltpu.SemaphoreType.DMA((2,)),
            pltpu.SemaphoreType.DMA,
        ],
        compiler_params=pltpu.CompilerParams(vmem_limit_bytes=LIMIT),
        cost_estimate=pl.CostEstimate(
            flops=2 * half * markers, bytes_accessed=half * markers, transcendentals=0
        ),
        name="front_a",
    )(pinned(kept_0), *in_hbm(effects), genotypes)


def front_b_kernel(n, n_src, kept_0_ref, kept_a_ref, *refs):
    small_any, g_hbm = refs[: n_src + 3], refs[n_src + 3]
    kept_ref, odd, rest = refs[n_src + 4 : n_src + 7]
    key_s, y_s, lane_s, sub_s, v_s, acc, tab, *small_s, sem, small_sem = refs[n_src + 7 :]
    quarter = kept_ref.shape[0] // (n // 4)
    half = quarter * n
    rows = quarter // LANES
    chain, rec, ani = lax.axis_index("chain"), lax.axis_index("rec"), lax.axis_index("ani")

    small = [
        pltpu.make_async_copy(a, b, small_sem.at[k])
        for k, (a, b) in enumerate(zip(small_any, small_s))
    ]
    for copy in small:
        copy.start()
    big = [load(2 * i, n, g_hbm, kept_ref, sem) for i in range(n // 4, n // 2)]
    for copy in big:
        copy.start()
    for copy in small:
        copy.wait()
    srcs, (*herds, gain_a) = small_s[:n_src], small_s[n_src:]

    most = compact(srcs, ani * 2 * half + chain * half, key_s, y_s)
    acc[...] = jnp.zeros_like(acc)
    lanes_iota = lax.broadcasted_iota(jnp.int32, (2 * LANES, LANES), 0).astype(F32).astype(BF16)
    subs_iota = lax.broadcasted_iota(jnp.int32, (SUBS, LANES), 0).astype(F32).astype(BF16)

    @pl.loop(0, (most + CHUNK_ROWS - 1) // CHUNK_ROWS)
    def _(t):
        look_up(t, herds, key_s, y_s, lane_s, sub_s, v_s)
        b, a = one_hots(t, lane_s, sub_s, v_s, lanes_iota, subs_iota)
        acc[...] += lax.dot_general(b, a, NT, preferred_element_type=F32)

    for q in range(n):
        wide, first = divmod(q * rows, SUBS)
        cols = slice(wide * LANES, (wide + 1) * LANES)
        window = lambda p: acc[p * SUBS + first : p * SUBS + first + rows, cols]
        tab[q, 0:rows, :] = window(0) + window(1)
        tab[q, rows : 2 * rows, :] = window(2) + window(3)
        tab[q, 2 * rows : 3 * rows, :] = window(4)
    for i in range(n // 2):
        rest[i] = tab[rec ^ (2 * i)]
        odd[i, 2 * rows : 5 * rows, :] = tab[rec ^ (2 * i + 1)]
        odd[i, 0 : 2 * rows, :] = gain_a[i]
    for copy in big:
        copy.wait()


def front_b(genotypes, kept, gain_a, herds, srcs, n):
    block, markers = genotypes.shape
    half = block // 2
    quarter = half // n
    total = len(srcs) * srcs[0].shape[0] // 3
    rows = quarter // LANES
    small = [*srcs, *herds, gain_a]
    return pl.pallas_call(
        functools.partial(front_b_kernel, n, len(srcs)),
        in_specs=[VMEM] * 2 + [ANY] * (1 + len(small)),
        out_specs=[VMEM] * 3,
        out_shape=[
            pltpu.VMEM((n // 4 * quarter, markers), BF16),
            jax.ShapeDtypeStruct((n // 2, 5 * rows, LANES), F32),
            jax.ShapeDtypeStruct((n // 2, 3 * rows, LANES), F32),
        ],
        scratch_shapes=[
            pltpu.VMEM((total, LANES), jnp.int32),
            pltpu.VMEM((total, LANES), F32),
            pltpu.VMEM((total, LANES), F32),
            pltpu.VMEM((total, LANES), F32),
            pltpu.VMEM((4, total, LANES), F32),
            pltpu.VMEM((5 * SUBS, 2 * LANES), F32),
            pltpu.VMEM((n, 3 * rows, LANES), F32),
        ]
        + [pltpu.VMEM(x.shape, F32) for x in small]
        + [pltpu.SemaphoreType.DMA((n // 4,)), pltpu.SemaphoreType.DMA((len(small),))],
        compiler_params=pltpu.CompilerParams(vmem_limit_bytes=LIMIT),
        cost_estimate=pl.CostEstimate(
            flops=4 * half * markers, bytes_accessed=half * markers, transcendentals=0
        ),
        name="front_b",
    )(
        *map(pinned, kept),
        *in_hbm(small),
        genotypes,
    )


def pinned(x):
    return pltpu.with_memory_space_constraint(x, pltpu.VMEM)


def front_c_kernel(n, kept_0_ref, kept_a_ref, kept_b_ref, rest_ref, *outs):
    quarter = kept_b_ref.shape[0] // (n // 4)
    rows = quarter // LANES
    e2 = kept_a_ref[n // 2 * quarter : n // 2 * quarter + 8, :]
    for i in range(n // 2):
        outs[i][2 * rows : 5 * rows, :] = rest_ref[i]
        late, slot = locate(2 * i, n)
        kept_ref = (kept_0_ref, kept_a_ref, kept_b_ref)[late]
        gains(e2, kept_ref, slot * quarter, quarter, outs[i], 0, rows)


def front_c(kept, rest, n):
    quarter, markers = kept[2].shape[0] // (n // 4), kept[2].shape[1]
    piece = jax.ShapeDtypeStruct((5 * quarter // LANES, LANES), F32)
    return pl.pallas_call(
        functools.partial(front_c_kernel, n),
        in_specs=[VMEM] * 4,
        out_specs=[VMEM] * (n // 2),
        out_shape=[piece] * (n // 2),
        compiler_params=pltpu.CompilerParams(vmem_limit_bytes=LIMIT),
        cost_estimate=pl.CostEstimate(
            flops=2 * n * quarter * markers, bytes_accessed=n * quarter * markers, transcendentals=0
        ),
        name="front_c",
    )(*map(pinned, kept), rest)


def merge_kernel(kept_0_ref, kept_a_ref, kept_b_ref, came_ref, *refs):
    count = len(refs) // 2
    for i in range(count):
        refs[count + i][...] = refs[i][...] + came_ref[i + 1]


def merge(kept, came, pieces):
    return pl.pallas_call(
        merge_kernel,
        in_specs=[VMEM] * (4 + len(pieces)),
        out_specs=[VMEM] * len(pieces),
        out_shape=[jax.ShapeDtypeStruct(x.shape, F32) for x in pieces],
        compiler_params=pltpu.CompilerParams(vmem_limit_bytes=LIMIT),
        cost_estimate=pl.CostEstimate(flops=1 << 16, bytes_accessed=1 << 16, transcendentals=0),
        name="merge",
    )(*map(pinned, kept), came, *pieces)


def combine_kernel(kept_0_ref, kept_a_ref, kept_b_ref, came_ref, *refs):
    parts, out_ref = refs[:-1], refs[-1]
    rows = out_ref.shape[0] // 2
    total = came_ref[0]
    for part in parts:
        total = total + part[...]
    count = total[4 * rows :]
    for ch in range(2):
        gain = total[ch * rows : (ch + 1) * rows]
        out_ref[ch * rows : (ch + 1) * rows, :] = (
            total[(2 + ch) * rows : (3 + ch) * rows] - count * gain
        )


def combine(kept, came, parts):
    rows = parts[0].shape[0] // 5
    return pl.pallas_call(
        combine_kernel,
        in_specs=[VMEM] * (4 + len(parts)),
        out_specs=VMEM,
        out_shape=jax.ShapeDtypeStruct((2 * rows, LANES), F32),
        compiler_params=pltpu.CompilerParams(vmem_limit_bytes=LIMIT),
        cost_estimate=pl.CostEstimate(flops=1 << 16, bytes_accessed=1 << 16, transcendentals=0),
        name="combine",
    )(*map(pinned, kept), came, *parts)


def product(n, kept_refs, js, parts):
    quarter = kept_refs[2].shape[0] // (n // 4)
    rows = quarter // LANES
    total = jnp.zeros((8, kept_refs[1].shape[1]), F32)
    for j, part in zip(js, parts):
        cols = [
            jnp.concatenate(
                [part[i : i + 1, :], part[rows + i : rows + i + 1, :], jnp.zeros((6, LANES), F32)],
                axis=0,
            )
            for i in range(rows)
        ]
        lhs = jnp.concatenate(cols, axis=1).astype(BF16)
        late, slot = locate(j, n)
        total = total + jnp.dot(
            lhs,
            kept_refs[late][slot * quarter : (slot + 1) * quarter, :],
            preferred_element_type=F32,
        )
    return total


def back_kernel(n, js, kept_0_ref, kept_a_ref, kept_b_ref, *refs):
    parts, before, out_ref = refs[: len(js)], refs[len(js) : -1], refs[-1]
    total = product(n, (kept_0_ref, kept_a_ref, kept_b_ref), js, parts)
    out_ref[...] = total + before[0][...] if before else total


def back(kept, js, parts, n, *before):
    quarter, markers = kept[2].shape[0] // (n // 4), kept[2].shape[1]
    return pl.pallas_call(
        functools.partial(back_kernel, n, js),
        in_specs=[VMEM] * (3 + len(js) + len(before)),
        out_specs=VMEM,
        out_shape=jax.ShapeDtypeStruct((8, markers), F32),
        compiler_params=pltpu.CompilerParams(vmem_limit_bytes=LIMIT),
        cost_estimate=pl.CostEstimate(
            flops=4 * quarter * markers * len(js),
            bytes_accessed=2 * quarter * markers * len(js),
            transcendentals=0,
        ),
        name="back",
    )(*map(pinned, kept), *parts, *before)


def back_last_kernel(n, js, kept_0_ref, kept_a_ref, kept_b_ref, before_ref, *refs):
    parts, (own_ref, theirs_ref) = refs[:n], refs[n:]
    e_rows = own_ref.shape[0]
    rows = parts[0].shape[0] // 2
    for j in range(n):
        at = e_rows + j * rows
        theirs_ref[at : at + rows, :] = parts[j][rows : 2 * rows, :]
    total = before_ref[...] + product(n, (kept_0_ref, kept_a_ref, kept_b_ref), js, [parts[j] for j in js])
    for i in range(own_ref.shape[0]):
        own_ref[i : i + 1, :] = total[0:1, i * LANES : (i + 1) * LANES]
        theirs_ref[i : i + 1, :] = total[1:2, i * LANES : (i + 1) * LANES]


def back_last(kept, js, parts, n, before):
    quarter, markers = kept[2].shape[0] // (n // 4), kept[2].shape[1]
    grad = jax.ShapeDtypeStruct((markers // LANES, LANES), F32)
    return pl.pallas_call(
        functools.partial(back_last_kernel, n, js),
        in_specs=[VMEM] * (4 + n),
        out_specs=[VMEM] * 2,
        out_shape=[
            grad,
            jax.ShapeDtypeStruct((markers // LANES + n * quarter // LANES, LANES), F32),
        ],
        compiler_params=pltpu.CompilerParams(vmem_limit_bytes=LIMIT),
        cost_estimate=pl.CostEstimate(
            flops=4 * quarter * markers * len(js),
            bytes_accessed=2 * quarter * markers * len(js),
            transcendentals=0,
        ),
        name="back_last",
    )(*map(pinned, kept), before, *parts)


def assemble_kernel(n, theirs_ref, *refs):
    parts, out_ref = refs[:n], refs[n]
    rows = parts[0].shape[0] // 2
    e_rows = theirs_ref.shape[0] - n * rows
    chain, rec = lax.axis_index("chain"), lax.axis_index("rec")
    for j in range(n):
        owner = rec ^ j
        out_ref[chain * n + owner] = parts[j][0:rows, :]
        out_ref[(1 - chain) * n + owner] = theirs_ref[
            e_rows + j * rows : e_rows + (j + 1) * rows, :
        ]


def assemble(theirs, parts, n):
    rows = parts[0].shape[0] // 2
    return pl.pallas_call(
        functools.partial(assemble_kernel, n),
        in_specs=[VMEM] * (1 + n),
        out_specs=VMEM,
        out_shape=jax.ShapeDtypeStruct((2 * n, rows, LANES), F32),
        cost_estimate=pl.CostEstimate(flops=1 << 16, bytes_accessed=1 << 18, transcendentals=0),
        name="assemble",
    )(theirs, *parts)


def on_device(
    n_rec,
    n_ani,
    genotypes,
    effects,
    gaussian_draw,
    prior_prec,
    accept,
    herd_effect,
    phenotype,
    record_animal,
    record_bin,
    live_records,
):
    step_size = 0.005
    n = n_rec

    effects_2d, herd_2d = tiled(effects), tiled(herd_effect)
    theirs = (swap(effects_2d, "chain", 2, 1), swap(herd_2d, "chain", 2, 1))
    kept_0, raw = prepare(
        genotypes,
        herd_effect.shape[0],
        n,
        live_records,
        tiled(record_animal),
        tiled(phenotype),
        tiled(record_bin),
    )
    theirs, raw = lax.optimization_barrier((theirs, raw))
    srcs = [raw] + [swap(raw, "ani", n_ani, j) for j in range(1, n_ani)]

    kept_a, gain_a = front_a(genotypes, kept_0, [effects_2d, theirs[0]], n)
    kept_b, odd, rest = front_b(genotypes, (kept_0, kept_a), gain_a, [herd_2d, theirs[1]], srcs, n)
    kept = (kept_0, kept_a, kept_b)
    came = swap(odd, "rec", n, 1)
    mine, *even = front_c(kept, rest, n)
    even = merge(kept, came, even)
    resid = combine(kept, came, [mine] + [swap(x, "rec", n, 2 * i + 2) for i, x in enumerate(even)])

    parts = [resid] + [swap(resid, "rec", n, j) for j in range(1, n)]
    grads = back(kept, [0], [resid], n)
    steps = [list(range(j, min(j + n // 4, n))) for j in range(1, n, n // 4)]
    for js in steps[:-1]:
        grads = back(kept, js, [parts[j] for j in js], n, grads)
    own, theirs = back_last(kept, steps[-1], parts, n, grads)
    swapped = swap(theirs, "chain", 2, 1)
    grad_part = own + swapped[: own.shape[0]]
    resid_sum = assemble(swapped, parts, n).reshape(-1)
    others = [shift(grad_part, "ani", n_ani, j) for j in range(1, n_ani)]

    likelihood_grad = grad_part
    for x in others:
        likelihood_grad = likelihood_grad + x
    likelihood_grad = likelihood_grad.reshape(-1)
    gradient = likelihood_grad - prior_prec * effects
    proposal = effects + step_size * gradient + math.sqrt(2.0 * step_size) * gaussian_draw
    accepted = jnp.repeat(accept, BLOCK) == 1
    return (jnp.where(accepted, proposal, effects), resid_sum)


def solution(mesh):
    return jax.shard_map(
        functools.partial(on_device, mesh.shape["rec"], mesh.shape["ani"]),
        mesh=mesh,
        in_specs=(
            P("ani", "rec"),
            P(("chain", "rec")),
            P(("chain", "rec")),
            P("rec"),
            P(("chain", "rec")),
            P(("chain", "rec")),
            P(("rec", "ani")),
            P(("rec", "ani")),
            P(("rec", "ani")),
            P(("rec", "ani")),
        ),
        out_specs=(P(("chain", "rec")), P(("chain", "ani"))),
        check_vma=False,
    )
```
